256 devices in a mesh: group: 8 (over y_lo, x), tile: 32 (over z, y_hi, core).
Axes of the slice: x: 4, y: 4 (y_hi: 2, y_lo: 2; y = y_hi * 2 + y_lo), z: 8, core: 2. Of those that a mesh axis runs over, the one named last changes fastest.
Arguments:
- state_in: bfloat16 [256, 200, 8, 128], P(('group', 'tile')), may hold values from -6 to 6
- cotangent: bfloat16 [256, 200, 8, 128], P(('group', 'tile')), may hold values from -6 to 6
- ocean_mask: int32 [256, 8, 128], P(('group', 'tile')), may hold values from 0 to 1, as said below
- slot_column: int32 [256], P(('group', 'tile')), may hold values from -1 to 0, as said below
- dw_taps: bfloat16 [200, 49], replicated, may hold values from -0.875 to 0.875
- dw_bias: bfloat16 [200], replicated, may hold values from -3 to 3
- norm_gain: bfloat16 [200], replicated, may hold values from 0.099609375 to 1.8984375
- norm_bias: bfloat16 [200], replicated, may hold values from -3 to 3
- up_weight: bfloat16 [800, 200], replicated, may hold values from -0.4375 to 0.4375
- up_bias: bfloat16 [800], replicated, may hold values from -3 to 3
- down_weight: bfloat16 [200, 800], replicated, may hold values from -0.21875 to 0.21875
- down_bias: bfloat16 [200], replicated, may hold values from -3 to 3
- layer_scale: bfloat16 [200], replicated, may hold values from 0.5 to 1.5
Outputs:
- grad_state: bfloat16 [256, 200, 8, 128], P(('group', 'tile'))
- grad_up: float32 [800, 200], P('tile')
- grad_up_bias: float32 [800], P('tile')
- grad_down: float32 [200, 800], P(None, 'tile')
- grad_taps: float32 [200, 49], replicated
- grad_vectors: float32 [5, 200], replicated
The draws below stay inside these ranges and needn't reach their ends.
Inputs may be any that keep to these rules, and one draw needn't show every extreme that they name: `slot_column`: on each device the slots hold, in increasing order, the columns of its block of 1 tile columns that carry ocean, then -1; a device may hold no tile, and in every band some device holds all 1. `ocean_mask`: all zero in slots whose column is -1.
All inputs are finite; a program needn't handle non-finite values.
Results may differ from the reference program's by a relative error of at most 0.0075.
Values may be sent and summed in bfloat16 or wider, within the bound.
A program may use at most 64 MiB of HBM per device.

```python
import math
import jax
import jax.numpy as jnp
from jax import lax

CHANNELS = 200
EXPANDED = 800
KERNEL = 7
TILE_ROWS = 8
TILE_COLS = 128
SLOTS_DEV = 1
BAND_COLUMNS = 32
ALL_SLOTS = 256


def ocean_layout(key):
    devices = ALL_SLOTS // SLOTS_DEV
    per_band = BAND_COLUMNS // SLOTS_DEV
    band_count = devices // per_band
    ocean_flags = jax.random.randint(jax.random.fold_in(key, 11), (devices, SLOTS_DEV), 0, 100) < 55
    positions = jnp.arange(SLOTS_DEV, dtype=jnp.int32)[None, :]
    chosen = jax.random.randint(jax.random.fold_in(key, 13), (band_count,), 0, per_band)
    full_device = jnp.arange(band_count, dtype=jnp.int32) * per_band + chosen
    whole_rows = jnp.zeros((devices,), jnp.int32).at[full_device].set(1) > 0
    ocean_flags = ocean_flags | whole_rows[:, None]
    order_key = jnp.where(ocean_flags, positions, positions + SLOTS_DEV)
    ordered = jnp.sort(order_key, axis=1)
    return jnp.where(ordered < SLOTS_DEV, ordered, -1).reshape(ALL_SLOTS).astype(jnp.int32)


def draw_slot_column(key, part):
    return ocean_layout(key)


def draw_ocean_mask(key, part):
    columns = ocean_layout(key)
    key = jax.random.fold_in(key, 21)
    ocean_share = jax.random.randint(jax.random.fold_in(key, 1), (ALL_SLOTS, 1, 1), 40, 101)
    cell_draw = jax.random.randint(jax.random.fold_in(key, 2), (ALL_SLOTS, TILE_ROWS, TILE_COLS), 0, 100)
    return ((cell_draw < ocean_share) & (columns >= 0)[:, None, None]).astype(jnp.int32)


def levels(key, dims, split, low, high):
    def one(axis_at, shards_of):
        steps = jax.random.uniform(jax.random.fold_in(jax.random.fold_in(key, 6), axis_at), (shards_of,), jnp.float32, low / len(split), high / len(split))
        return jnp.repeat(jnp.exp(steps), dims[axis_at] // shards_of).reshape((-1,) + (1,) * (len(dims) - axis_at - 1))

    gain = one(*split[0])
    for cut in split[1:]:
        gain = gain * one(*cut)
    return gain


def scatter_about(stream_key, extent, scale, most, shards=(), kind=jnp.bfloat16):
    level = levels(stream_key, extent, shards, -0.22, 0.18) if shards else 1.0
    entries = jax.random.normal(stream_key, extent, jnp.float32) * scale * level
    return jnp.minimum(jnp.maximum(entries, -most), most).astype(kind)


def setup_inputs(seed: int = 0) -> dict:
    keys = jax.random.split(jax.random.key(seed), 14)
    state_in = scatter_about(keys[0], (ALL_SLOTS, CHANNELS, TILE_ROWS, TILE_COLS), 1.0, 6.0, ((0, 256),))
    cotangent = scatter_about(keys[1], (ALL_SLOTS, CHANNELS, TILE_ROWS, TILE_COLS), 1.0, 6.0, ((0, 256),))
    ocean_mask = draw_ocean_mask(jax.random.fold_in(keys[13], 71), 0)
    slot_column = draw_slot_column(jax.random.fold_in(keys[13], 71), 0)
    dw_taps = scatter_about(keys[4], (CHANNELS, KERNEL * KERNEL), (KERNEL * KERNEL) ** -0.5, 0.875)
    dw_bias = scatter_about(keys[5], (CHANNELS,), 0.5, 3.0)
    norm_gain = jnp.clip(1.0 + 0.18 * jax.random.normal(keys[6], (CHANNELS,), jnp.float32), 0.099609375, 1.8984375).astype(jnp.bfloat16)
    norm_bias = scatter_about(keys[7], (CHANNELS,), 0.5, 3.0)
    up_weight = scatter_about(keys[8], (EXPANDED, CHANNELS), CHANNELS ** -0.5, 0.4375)
    up_bias = scatter_about(keys[9], (EXPANDED,), 0.5, 3.0)
    down_weight = scatter_about(keys[10], (CHANNELS, EXPANDED), EXPANDED ** -0.5, 0.21875)
    down_bias = scatter_about(keys[11], (CHANNELS,), 0.5, 3.0)
    layer_scale = jnp.clip(jax.random.uniform(keys[12], (CHANNELS,), jnp.float32, 0.5, 1.5), 0.5, 1.5).astype(jnp.bfloat16)
    return dict(state_in=state_in, cotangent=cotangent, ocean_mask=ocean_mask, slot_column=slot_column, dw_taps=dw_taps, dw_bias=dw_bias, norm_gain=norm_gain, norm_bias=norm_bias, up_weight=up_weight, up_bias=up_bias, down_weight=down_weight, down_bias=down_bias, layer_scale=layer_scale)


NORM_EPSILON = 1e-06
SQRT_HALF = 0.7071067811865476
GAUSS_SCALE = 0.3989422804014327

def gelu_parts(values):
    lower_mass = 0.5 * (1.0 + lax.erf(values * SQRT_HALF))
    density = GAUSS_SCALE * jnp.exp(-0.5 * values * values)
    return (values * lower_mass, lower_mass + values * density)

def depthwise(extended, dw_taps, flipped):
    height = extended.shape[1] - KERNEL + 1
    breadth = extended.shape[2] - KERNEL + 1
    source = extended.astype(jnp.float32)
    taps_wide = dw_taps.astype(jnp.float32)
    summed = jnp.zeros((extended.shape[0], height, breadth), jnp.float32)
    for row_tap in range(KERNEL):
        for col_tap in range(KERNEL):
            row_start = KERNEL - 1 - row_tap if flipped else row_tap
            col_start = KERNEL - 1 - col_tap if flipped else col_tap
            weight = taps_wide[:, row_tap * KERNEL + col_tap][:, None, None]
            summed = summed + weight * source[:, row_start:row_start + height, col_start:col_start + breadth]
    return summed

def tap_grads(extended, own_grad):
    height = own_grad.shape[1]
    breadth = own_grad.shape[2]
    source = extended.astype(jnp.float32)
    columns = []
    for row_tap in range(KERNEL):
        for col_tap in range(KERNEL):
            columns.append(lax.optimization_barrier(jnp.sum(own_grad * source[:, row_tap:row_tap + height, col_tap:col_tap + breadth], axis=(1, 2))))
    return jnp.stack(columns, axis=1)

def slot_forward_backward(extended, mask_cells, upstream, dw_taps, dw_bias, norm_gain, norm_bias, up_weight, up_bias, down_weight, down_bias, layer_scale):
    channel_count = extended.shape[0]
    conv_out = depthwise(extended, dw_taps, False) + dw_bias.astype(jnp.float32)[:, None, None]
    height = conv_out.shape[1]
    breadth = conv_out.shape[2]
    cell_count = height * breadth
    conv_low = conv_out.astype(jnp.bfloat16).reshape(channel_count, cell_count)
    conv_wide = conv_low.astype(jnp.float32)
    center = lax.optimization_barrier(jnp.mean(conv_wide, axis=0, keepdims=True))
    offset = conv_wide - center
    spread = lax.rsqrt(lax.optimization_barrier(jnp.mean(offset * offset, axis=0, keepdims=True)) + NORM_EPSILON)
    normed = offset * spread
    gain_col = norm_gain.astype(jnp.float32)[:, None]
    normed_low = (normed * gain_col + norm_bias.astype(jnp.float32)[:, None]).astype(jnp.bfloat16)
    hidden_pre = jnp.dot(up_weight, normed_low, preferred_element_type=jnp.float32) + up_bias.astype(jnp.float32)[:, None]
    activated, derivative = gelu_parts(hidden_pre)
    activated_low = activated.astype(jnp.bfloat16)
    branch = jnp.dot(down_weight, activated_low, preferred_element_type=jnp.float32) + down_bias.astype(jnp.float32)[:, None]
    mask_row = mask_cells.astype(jnp.float32).reshape(1, cell_count)
    masked_grad = upstream.astype(jnp.float32).reshape(channel_count, cell_count) * mask_row
    grad_scale = lax.optimization_barrier(jnp.sum(masked_grad * branch, axis=1))
    grad_branch = layer_scale.astype(jnp.float32)[:, None] * masked_grad
    grad_branch_low = grad_branch.astype(jnp.bfloat16)
    grad_down_bias = lax.optimization_barrier(jnp.sum(grad_branch, axis=1))
    grad_down = lax.dot_general(grad_branch_low, activated_low, (((1,), (1,)), ((), ())), preferred_element_type=jnp.float32)
    grad_act = lax.dot_general(down_weight, grad_branch_low, (((0,), (0,)), ((), ())), preferred_element_type=jnp.float32)
    grad_pre = grad_act * derivative
    grad_pre_low = grad_pre.astype(jnp.bfloat16)
    grad_up_bias = lax.optimization_barrier(jnp.sum(grad_pre, axis=1))
    grad_up = lax.dot_general(grad_pre_low, normed_low, (((1,), (1,)), ((), ())), preferred_element_type=jnp.float32)
    grad_normed = lax.dot_general(up_weight, grad_pre_low, (((0,), (0,)), ((), ())), preferred_element_type=jnp.float32)
    grad_gain = lax.optimization_barrier(jnp.sum(grad_normed * normed, axis=1))
    grad_shift = lax.optimization_barrier(jnp.sum(grad_normed, axis=1))
    scaled = grad_normed * gain_col
    grad_conv = spread * (scaled - lax.optimization_barrier(jnp.mean(scaled, axis=0, keepdims=True)) - normed * lax.optimization_barrier(jnp.mean(scaled * normed, axis=0, keepdims=True)))
    grad_conv_low = grad_conv.astype(jnp.bfloat16).reshape(channel_count, height, breadth)
    return (grad_conv_low, (grad_up, grad_up_bias, grad_down, grad_down_bias, grad_scale, grad_gain, grad_shift))

def slot_finish(grad_extended, extended, mask_cells, upstream, dw_taps):
    margin = KERNEL // 2
    height = mask_cells.shape[0]
    breadth = mask_cells.shape[1]
    conv_part = depthwise(grad_extended, dw_taps, True)
    mask_wide = mask_cells.astype(jnp.float32)[None]
    direct = upstream.astype(jnp.float32) * mask_wide
    grad_in = (mask_wide * (direct + conv_part)).astype(jnp.bfloat16)
    own_grad = grad_extended[:, margin:margin + height, margin:margin + breadth].astype(jnp.float32)
    return (grad_in, tap_grads(extended, own_grad), lax.optimization_barrier(jnp.sum(own_grad, axis=(1, 2))))

def slot_places(slot_column):
    slot_index = jnp.arange(ALL_SLOTS, dtype=jnp.int32)
    device_index = slot_index // SLOTS_DEV
    per_band = BAND_COLUMNS // SLOTS_DEV
    band_index = device_index // per_band
    column_index = device_index % per_band * SLOTS_DEV + jnp.maximum(slot_column, 0)
    return (band_index, column_index)

def extend_all(slot_field, band_index, column_index):
    margin = KERNEL // 2
    band_count = ALL_SLOTS // BAND_COLUMNS
    band_grid = jnp.zeros((band_count, BAND_COLUMNS) + slot_field.shape[1:], slot_field.dtype)
    band_grid = band_grid.at[band_index, column_index].add(slot_field)
    width_dim = slot_field.shape[1]
    grid_plane = band_grid.transpose(2, 0, 3, 1, 4).reshape(width_dim, band_count * TILE_ROWS, BAND_COLUMNS * TILE_COLS)
    grid_plane = jnp.concatenate([grid_plane[:, :, -margin:], grid_plane, grid_plane[:, :, :margin]], axis=2)
    return jnp.pad(grid_plane, ((0, 0), (margin, margin), (0, 0)))

def window(grid_plane, band_index, column_index, live_slot, slot_index):
    margin = KERNEL // 2
    start_row = band_index[slot_index] * TILE_ROWS
    start_col = column_index[slot_index] * TILE_COLS
    window_cut = lax.dynamic_slice(grid_plane, (jnp.int32(0), start_row, start_col), (grid_plane.shape[0], TILE_ROWS + 2 * margin, TILE_COLS + 2 * margin))
    return window_cut * live_slot[slot_index].astype(window_cut.dtype)

def reference(state_in, cotangent, ocean_mask, slot_column, dw_taps, dw_bias, norm_gain, norm_bias, up_weight, up_bias, down_weight, down_bias, layer_scale):
    band_index, column_index = slot_places(slot_column)
    live_slot = (slot_column >= 0).astype(jnp.int32)
    masked_state = state_in * ocean_mask.astype(jnp.bfloat16)[:, None]
    state_plane = extend_all(masked_state, band_index, column_index)
    zero_parts = (jnp.zeros(up_weight.shape, jnp.float32), jnp.zeros(up_bias.shape, jnp.float32), jnp.zeros(down_weight.shape, jnp.float32), jnp.zeros(down_bias.shape, jnp.float32), jnp.zeros(down_bias.shape, jnp.float32), jnp.zeros(down_bias.shape, jnp.float32), jnp.zeros(down_bias.shape, jnp.float32))

    def first_pass(running, slot_index):
        extended = window(state_plane, band_index, column_index, live_slot, slot_index)
        grad_conv_low, partials = slot_forward_backward(extended, ocean_mask[slot_index], cotangent[slot_index], dw_taps, dw_bias, norm_gain, norm_bias, up_weight, up_bias, down_weight, down_bias, layer_scale)
        return (jax.tree.map(jnp.add, running, partials), grad_conv_low)
    slot_order = jnp.arange(ALL_SLOTS, dtype=jnp.int32)
    totals, grad_conv_all = lax.scan(first_pass, zero_parts, slot_order)
    grad_plane = extend_all(grad_conv_all, band_index, column_index)

    def second_pass(running, slot_index):
        extended = window(state_plane, band_index, column_index, live_slot, slot_index)
        grad_extended = window(grad_plane, band_index, column_index, live_slot, slot_index)
        grad_in, taps_part, bias_part = slot_finish(grad_extended, extended, ocean_mask[slot_index], cotangent[slot_index], dw_taps)
        return ((running[0] + taps_part, running[1] + bias_part), grad_in)
    start_sums = (jnp.zeros(dw_taps.shape, jnp.float32), jnp.zeros(dw_bias.shape, jnp.float32))
    (taps_sum, bias_sum), grad_state = lax.scan(second_pass, start_sums, slot_order)
    factor = 1.0 / math.sqrt(ALL_SLOTS * TILE_ROWS * TILE_COLS)
    grad_up, grad_up_bias, grad_down, grad_down_bias, grad_scale, grad_gain, grad_shift = totals
    grad_vectors = jnp.stack([bias_sum, grad_gain, grad_shift, grad_down_bias, grad_scale], axis=0) * factor
    return (grad_state, grad_up * factor, grad_up_bias * factor, grad_down * factor, taps_sum * factor, grad_vectors)
```

```python
import functools
import math

import jax
import jax.numpy as jnp
from jax import lax
from jax.experimental import pallas as pl
from jax.experimental.pallas import tpu as pltpu
from jax.sharding import PartitionSpec as P

MESH = pl.DeviceIdType.MESH
F32 = jnp.float32
BF16 = jnp.bfloat16

CHANNELS = 200
PADDED = 208
HIDDEN = 800
KERNEL = 7
TAPS = KERNEL * KERNEL
MARGIN = 3
ROWS = 8
COLS = 128
CELLS = ROWS * COLS
TALL = ROWS + 2 * MARGIN
BLOCKS = CHANNELS // 8
FOLD = 104
GROUPS = 8
TILES = 32
CHIPS = TILES // 2
SHARE = HIDDEN // TILES
CHUNK = 80

NORM_EPSILON = 1e-06
SQRT_HALF = 0.7071067811865476
GAUSS_SCALE = 0.3989422804014327

DW_BIAS, GAIN, SHIFT, DOWN_BIAS, SCALE = range(TAPS, TAPS + 5)


def lanes_of(shape):
    return lax.broadcasted_iota(jnp.int32, shape, len(shape) - 1)


def source_row(row):
    if row < MARGIN:
        return 1, row + ROWS - MARGIN
    if row < MARGIN + ROWS:
        return 0, row - MARGIN
    return 2, row - MARGIN - ROWS


def shifted_rows(ext, sides, rows, column):
    move = column - MARGIN
    lane = lanes_of((8, COLS))
    out = []
    for row in range(TALL):
        main = ext[row, rows, :]
        if move > 0:
            main = pltpu.roll(jnp.where(lane < move, sides[row], main), COLS - move, 1)
        elif move < 0:
            main = pltpu.roll(jnp.where(lane >= COLS + move, sides[row], main), -move, 1)
        out.append(main)
    return out


def side_rows(packs, rows):
    out = []
    for row in range(TALL):
        pack, origin = source_row(row)
        turn = (COLS - 8 * origin) % COLS
        side = packs[pack, rows, :]
        out.append(pltpu.roll(side, turn, 1) if turn else side)
    return out


def convolve(ext, packs, taps, rows, flipped, keep=None):
    sides = side_rows(packs, rows)
    total = [None] * ROWS
    for column in range(KERNEL):
        moved = shifted_rows(ext, sides, rows, column)
        if keep is not None:
            for row in range(TALL):
                keep[column, row, rows, :] = moved[row]
        for tap_row in range(KERNEL):
            index = tap_row * KERNEL + column
            weight = taps[TAPS - 1 - index if flipped else index, rows, :]
            for row in range(ROWS):
                term = weight * moved[row + tap_row]
                total[row] = term if total[row] is None else total[row] + term
    return total


def block_rows(block):
    return pl.ds(pl.multiple_of(block * 8, 8), 8)


def lane_slice(row):
    return pl.ds(pl.multiple_of(row * COLS, COLS), COLS)


def kernel(
    slot_ref,
    mask_ref,
    state_ref,
    cot_ref,
    cols_ref,
    upw_ref,
    downw_ref,
    gs_ref,
    tail_ref,
    flat,
    ext,
    exg,
    packs_s,
    packs_g,
    taps,
    kept,
    normed,
    spread,
    mgrad,
    nlow,
    gblow,
    act,
    gpre,
    branch,
    gnorm,
    up_t,
    down_t,
    gup,
    gdown,
    sums,
    small_wide,
    gstate,
    rows_send,
    rows_recv,
    pack_send,
    pack_recv,
    w_send,
    w_core,
    w_group,
    w_group_in,
    small,
    small_core,
    small_group,
    small_group_in,
    tile_send,
    tile_in,
    final,
    halo_ssem,
    halo_rsem,
    core_ssem,
    core_rsem,
    wgroup_ssem,
    wgroup_rsem,
    sgroup_ssem,
    sgroup_rsem,
    tile_ssem,
    tile_rsem,
    final_ssem,
    final_rsem,
):
    g = lax.axis_index("group")
    t = lax.axis_index("tile")
    core = lax.rem(t, 2)
    chip = t // 2
    partner = chip * 2 + 1 - core
    east = lax.rem(t + 1, TILES)
    west = lax.rem(t + TILES - 1, TILES)
    has_above = g > 0
    has_below = g < GROUPS - 1

    barrier = pltpu.get_barrier_semaphore()

    def greet(gg, tt):
        pl.semaphore_signal(barrier, inc=1, device_id=(gg, tt), device_id_type=MESH)

    greet(g, partner)
    greet(g, east)
    greet(g, west)
    for k in range(1, GROUPS):
        greet(lax.rem(g + k, GROUPS), t)
    for k in range(1, CHIPS):
        greet(g, lax.rem(chip + k, CHIPS) * 2 + core)

    @pl.when(has_above)
    def _():
        greet(g - 1, east)
        greet(g - 1, west)

    @pl.when(has_below)
    def _():
        greet(g + 1, east)
        greet(g + 1, west)

    def halo_copies(phase):
        def rows_copy(slot, gg):
            return pltpu.make_async_remote_copy(
                src_ref=rows_send.at[phase, slot],
                dst_ref=rows_recv.at[phase, slot],
                send_sem=halo_ssem.at[phase, slot],
                recv_sem=halo_rsem.at[phase, slot],
                device_id=(gg, t),
                device_id_type=MESH,
            )

        def pack_copy(slot, gg, tt):
            return pltpu.make_async_remote_copy(
                src_ref=pack_send.at[phase],
                dst_ref=pack_recv.at[phase, slot],
                send_sem=halo_ssem.at[phase, 2 + slot],
                recv_sem=halo_rsem.at[phase, 2 + slot],
                device_id=(gg, tt),
                device_id_type=MESH,
            )

        side = [pack_copy(0, g, west), pack_copy(1, g, east)]
        down = [rows_copy(0, g + 1), pack_copy(2, g + 1, west), pack_copy(3, g + 1, east)]
        up = [rows_copy(1, g - 1), pack_copy(4, g - 1, west), pack_copy(5, g - 1, east)]
        return side, down, up

    def halo_start(phase):
        side, down, up = halo_copies(phase)

        @pl.when(has_below)
        def _():
            for copy in down:
                copy.start()

        @pl.when(has_above)
        def _():
            for copy in up:
                copy.start()

        for copy in side:
            copy.start()

    def halo_wait(phase):
        side, down, up = halo_copies(phase)
        for copy in side:
            copy.wait_send()
            copy.wait_recv()

        @pl.when(has_below)
        def _():
            for copy in down:
                copy.wait_send()
            for copy in up:
                copy.wait_recv()

        @pl.when(has_above)
        def _():
            for copy in up:
                copy.wait_send()
            for copy in down:
                copy.wait_recv()

    def pack_up(phase, field):
        lane = lanes_of((CHANNELS, COLS))
        spot = lax.rem(lane + 3, COLS) // 8
        pack = field[MARGIN]
        for row in range(1, ROWS):
            pack = jnp.where(spot == row, pltpu.roll(field[MARGIN + row], 8 * row, 1), pack)
        second = pltpu.roll(pack[FOLD:], 64, 1)
        lane = lanes_of((CHANNELS - FOLD, COLS))
        first = jnp.where((lane >= 61) & (lane < 125), second, pack[: CHANNELS - FOLD])
        zeros = jnp.zeros((8, COLS), F32)
        whole = jnp.concatenate([first, pack[CHANNELS - FOLD : FOLD], zeros], axis=0)
        pack_send[phase] = whole.astype(BF16)
        pad = jnp.zeros((MARGIN, PADDED - CHANNELS, COLS), BF16)
        bottom = field[ROWS : ROWS + MARGIN].astype(BF16)
        top = field[MARGIN : 2 * MARGIN].astype(BF16)
        rows_send[phase, 0] = jnp.concatenate([bottom, pad], axis=1)
        rows_send[phase, 1] = jnp.concatenate([top, pad], axis=1)

    def unpack(phase, field, packs):
        field[:MARGIN] = rows_recv[phase, 0].astype(F32)[:, :CHANNELS]
        field[MARGIN + ROWS :] = rows_recv[phase, 1].astype(F32)[:, :CHANNELS]
        lane = lanes_of((112, COLS))
        for index in range(3):
            from_east = pack_recv[phase, 2 * index].astype(F32)
            from_west = pack_recv[phase, 2 * index + 1].astype(F32)
            both = jnp.where(lax.rem(lane, 8) < 4, from_east, from_west)
            packs[index, :FOLD, :] = both[:FOLD]
            packs[index, FOLD:, :] = pltpu.roll(both[: CHANNELS - FOLD], 64, 1)

    @pl.when(jnp.logical_not(has_above))
    def _():
        for phase in range(2):
            rows_recv[phase, 0] = jnp.zeros((MARGIN, PADDED, COLS), BF16)
            pack_recv[phase, 2] = jnp.zeros((112, COLS), BF16)
            pack_recv[phase, 3] = jnp.zeros((112, COLS), BF16)

    @pl.when(jnp.logical_not(has_below))
    def _():
        for phase in range(2):
            rows_recv[phase, 1] = jnp.zeros((MARGIN, PADDED, COLS), BF16)
            pack_recv[phase, 4] = jnp.zeros((112, COLS), BF16)
            pack_recv[phase, 5] = jnp.zeros((112, COLS), BF16)

    live = (slot_ref[0] >= 0).astype(F32)
    mask = mask_ref[...].astype(F32) * live
    flat[...] = (state_ref[...].astype(F32) * mask[None]).reshape(CHANNELS * ROWS, COLS)
    for row in range(ROWS):
        ext[MARGIN + row] = flat[pl.ds(row, CHANNELS, stride=ROWS), :]
    pack_up(0, ext)
    met = 3 + (GROUPS - 1) + (CHIPS - 1)
    met = met + 2 * has_above.astype(jnp.int32) + 2 * has_below.astype(jnp.int32)
    pl.semaphore_wait(barrier, met)
    halo_start(0)

    flat[...] = (cot_ref[...].astype(F32) * mask[None]).reshape(CHANNELS * ROWS, COLS)
    scale_col = cols_ref[:, SCALE : SCALE + 1]
    for row in range(ROWS):
        masked = flat[pl.ds(row, CHANNELS, stride=ROWS), :]
        mgrad[row] = masked
        gblow[:, row * COLS : (row + 1) * COLS] = (masked * scale_col).astype(BF16)
    for tap in range(TAPS):
        taps[tap] = jnp.broadcast_to(cols_ref[:, tap : tap + 1], (CHANNELS, COLS))
    up_t[...] = upw_ref[...].T
    down_t[...] = downw_ref[...].T

    halo_wait(0)
    unpack(0, ext, packs_s)

    @pl.loop(0, BLOCKS)
    def _(block):
        rows = block_rows(block)
        total = convolve(ext, packs_s, taps, rows, False, kept)
        bias = cols_ref[rows, DW_BIAS : DW_BIAS + 1]
        for row in range(ROWS):
            normed[row, rows, :] = (total[row] * live + bias).astype(BF16).astype(F32)

    gain_col = cols_ref[:, GAIN : GAIN + 1]
    shift_col = cols_ref[:, SHIFT : SHIFT + 1]

    @pl.loop(0, ROWS)
    def _(row):
        conv = normed[row]
        offset = conv - jnp.mean(conv, axis=0, keepdims=True)
        rate = lax.rsqrt(jnp.mean(offset * offset, axis=0, keepdims=True) + NORM_EPSILON)
        unit = offset * rate
        spread[row] = rate
        normed[row] = unit
        low = (unit * gain_col + shift_col).astype(BF16)
        tail = (lax.broadcasted_iota(jnp.int32, (PADDED - CHANNELS, COLS), 0) == 0).astype(BF16)
        nlow[:, lane_slice(row)] = jnp.concatenate([low, tail], axis=0)

    @pl.loop(0, HIDDEN // CHUNK)
    def _(chunk):
        units = pl.ds(pl.multiple_of(chunk * CHUNK, CHUNK), CHUNK)
        pre = jnp.dot(upw_ref[units, :], nlow[...], preferred_element_type=F32)
        mass = 0.5 * (1.0 + lax.erf(pre * SQRT_HALF))
        density = GAUSS_SCALE * jnp.exp(-0.5 * pre * pre)
        act[units, :] = (pre * mass).astype(BF16)
        grad_act = jnp.dot(down_t[units, :], gblow[...], preferred_element_type=F32)
        gpre[units, :] = (grad_act * (mass + pre * density)).astype(BF16)

    branch[...] = jnp.dot(downw_ref[...], act[...], preferred_element_type=F32)
    gnorm[...] = jnp.dot(up_t[...], gpre[...], preferred_element_type=F32)[:CHANNELS]

    sums[...] = jnp.zeros_like(sums)
    down_bias = cols_ref[:, DOWN_BIAS : DOWN_BIAS + 1]

    @pl.loop(0, ROWS)
    def _(row):
        grad = gnorm[:, lane_slice(row)]
        unit = normed[row]
        masked = mgrad[row]
        sums[1] += grad * unit
        sums[2] += grad
        sums[3] += masked * scale_col
        sums[4] += masked * (branch[:, lane_slice(row)] + down_bias)
        scaled = grad * gain_col
        first = jnp.mean(scaled, axis=0, keepdims=True)
        second = jnp.mean(scaled * unit, axis=0, keepdims=True)
        low = (spread[row] * (scaled - first - unit * second)).astype(BF16).astype(F32)
        exg[MARGIN + row] = low
        sums[0] += low

    pack_up(1, exg)
    halo_start(1)

    trans = (((1,), (1,)), ((), ()))
    gup[:HIDDEN, :PADDED] = lax.dot_general(gpre[...], nlow[...], trans, preferred_element_type=F32)
    gdown[:HIDDEN, :CHANNELS] = lax.dot_general(
        act[...], gblow[...], trans, preferred_element_type=F32
    )
    for tile in range(TILES):
        for half in range(2):
            begin = tile * SHARE + 16 * half
            size = 16
            if begin + size > HIDDEN:
                size = HIDDEN - begin
            for part in range(4):
                source = gup if part < 2 else gdown
                side = (part % 2) * COLS
                if size < 16:
                    piece = source[begin : begin + 16, side : side + COLS]
                    keep = lax.broadcasted_iota(jnp.int32, (16, COLS), 0) < size
                    piece = jnp.where(keep, piece, 0.0)
                else:
                    piece = source[begin : begin + 16, side : side + COLS]
                w_send[tile % 2, half * 4 + part, tile // 2] = piece.astype(BF16)

    w_core_copy = pltpu.make_async_remote_copy(
        src_ref=w_send.at[1 - core],
        dst_ref=w_core,
        send_sem=core_ssem.at[0],
        recv_sem=core_rsem.at[0],
        device_id=(g, partner),
        device_id_type=MESH,
    )
    w_core_copy.start()

    def tap_block(block):
        rows = block_rows(block)
        lane = lanes_of((8, COLS))
        own = [exg[MARGIN + row, rows, :] for row in range(ROWS)]
        out = jnp.zeros((8, COLS), F32)
        for column in range(KERNEL):
            moved = [kept[column, row, rows, :] for row in range(TALL)]
            for tap_row in range(KERNEL):
                total = own[0] * moved[tap_row]
                for row in range(1, ROWS):
                    total = total + own[row] * moved[row + tap_row]
                out = jnp.where(
                    lane == tap_row * KERNEL + column, jnp.sum(total, axis=1, keepdims=True), out
                )
        for vector in range(5):
            total = jnp.sum(sums[vector, rows, :], axis=1, keepdims=True)
            out = jnp.where(lane == TAPS + vector, total, out)
        small_wide[rows, :] = out * live

    def finish_block(block):
        rows = block_rows(block)
        total = convolve(exg, packs_g, taps, rows, True)
        for row in range(ROWS):
            cell = mask[row : row + 1]
            gstate[row, rows, :] = cell * (mgrad[row, rows, :] + total[row])

    pl.loop(0, BLOCKS // 2)(tap_block)

    w_core_copy.wait_send()
    w_core_copy.wait_recv()

    @pl.loop(0, GROUPS)
    def _(piece):
        total = w_send[core, piece].astype(F32) + w_core[piece].astype(F32)
        w_group[piece] = total.astype(BF16)

    def w_group_copy(k):
        other = lax.rem(g + k, GROUPS)
        return pltpu.make_async_remote_copy(
            src_ref=w_group.at[other],
            dst_ref=w_group_in.at[k],
            send_sem=wgroup_ssem.at[k],
            recv_sem=wgroup_rsem.at[k],
            device_id=(other, t),
            device_id_type=MESH,
        )

    for k in range(1, GROUPS):
        w_group_copy(k).start()

    pl.loop(BLOCKS // 2, BLOCKS)(tap_block)

    small[:FOLD] = small_wide[:FOLD]
    small[FOLD:] = jnp.zeros((128 - FOLD, COLS), F32)
    small[: CHANNELS - FOLD] += pltpu.roll(small_wide[FOLD:], 64, 1)
    s_core_copy = pltpu.make_async_remote_copy(
        src_ref=small,
        dst_ref=small_core,
        send_sem=core_ssem.at[1],
        recv_sem=core_rsem.at[1],
        device_id=(g, partner),
        device_id_type=MESH,
    )
    s_core_copy.start()

    halo_wait(1)
    unpack(1, exg, packs_g)
    pl.loop(0, BLOCKS // 2)(finish_block)

    s_core_copy.wait_send()
    s_core_copy.wait_recv()
    small_group[...] = (small[...] + small_core[...]).reshape(GROUPS, 16, COLS)

    def s_group_copy(k):
        other = lax.rem(g + k, GROUPS)
        return pltpu.make_async_remote_copy(
            src_ref=small_group.at[other],
            dst_ref=small_group_in.at[k],
            send_sem=sgroup_ssem.at[k],
            recv_sem=sgroup_rsem.at[k],
            device_id=(other, t),
            device_id_type=MESH,
        )

    for k in range(1, GROUPS):
        s_group_copy(k).start()

    pl.loop(BLOCKS // 2, BLOCKS)(finish_block)
    gs_ref[...] = gstate[...].astype(BF16)

    total = w_group[g].astype(F32)
    for k in range(1, GROUPS):
        w_group_copy(k).wait_send()
        w_group_copy(k).wait_recv()
        total = total + w_group_in[k].astype(F32)
    tile_send[:, 0] = total.astype(BF16)
    total = small_group[g]
    for k in range(1, GROUPS):
        s_group_copy(k).wait_send()
        s_group_copy(k).wait_recv()
        total = total + small_group_in[k]
    low = total.astype(BF16)
    for other in range(CHIPS):
        tile_send[other, 1] = low

    def tile_copy(k):
        other = lax.rem(chip + k, CHIPS)
        return pltpu.make_async_remote_copy(
            src_ref=tile_send.at[other],
            dst_ref=tile_in.at[chip],
            send_sem=tile_ssem.at[k],
            recv_sem=tile_rsem.at[k],
            device_id=(g, other * 2 + core),
            device_id_type=MESH,
        )

    for k in range(1, CHIPS):
        tile_copy(k).start()
    tile_in[chip] = tile_send[chip]
    for k in range(1, CHIPS):
        tile_copy(k).wait_send()
        tile_copy(k).wait_recv()
    total = tile_in[0].astype(F32)
    for other in range(1, CHIPS):
        total = total + tile_in[other].astype(F32)
    final[g] = total

    def final_copy(k):
        other = lax.rem(g + k, GROUPS)
        return pltpu.make_async_remote_copy(
            src_ref=final.at[g],
            dst_ref=final.at[g],
            send_sem=final_ssem.at[k],
            recv_sem=final_rsem.at[k],
            device_id=(other, t),
            device_id_type=MESH,
        )

    for k in range(1, GROUPS):
        final_copy(k).start()
    for k in range(1, GROUPS):
        final_copy(k).wait_send()
        final_copy(k).wait_recv()
    tail_ref[...] = final[...] * (1.0 / math.sqrt(CELLS * GROUPS * TILES))


def scratch():
    dma = pltpu.SemaphoreType.DMA
    return [
        pltpu.VMEM((CHANNELS * ROWS, COLS), F32),
        pltpu.VMEM((TALL, CHANNELS, COLS), F32),
        pltpu.VMEM((TALL, CHANNELS, COLS), F32),
        pltpu.VMEM((3, CHANNELS, COLS), F32),
        pltpu.VMEM((3, CHANNELS, COLS), F32),
        pltpu.VMEM((TAPS, CHANNELS, COLS), F32),
        pltpu.VMEM((KERNEL, TALL, CHANNELS, COLS), F32),
        pltpu.VMEM((ROWS, CHANNELS, COLS), F32),
        pltpu.VMEM((ROWS, 1, COLS), F32),
        pltpu.VMEM((ROWS, CHANNELS, COLS), F32),
        pltpu.VMEM((PADDED, CELLS), BF16),
        pltpu.VMEM((CHANNELS, CELLS), BF16),
        pltpu.VMEM((HIDDEN, CELLS), BF16),
        pltpu.VMEM((HIDDEN, CELLS), BF16),
        pltpu.VMEM((CHANNELS, CELLS), F32),
        pltpu.VMEM((CHANNELS, CELLS), F32),
        pltpu.VMEM((PADDED, HIDDEN), BF16),
        pltpu.VMEM((HIDDEN, CHANNELS), BF16),
        pltpu.VMEM((HIDDEN + 8, 256), F32),
        pltpu.VMEM((HIDDEN + 8, 256), F32),
        pltpu.VMEM((5, CHANNELS, COLS), F32),
        pltpu.VMEM((CHANNELS, COLS), F32),
        pltpu.VMEM((ROWS, CHANNELS, COLS), F32),
        pltpu.VMEM((2, 2, MARGIN, PADDED, COLS), BF16),
        pltpu.VMEM((2, 2, MARGIN, PADDED, COLS), BF16),
        pltpu.VMEM((2, 112, COLS), BF16),
        pltpu.VMEM((2, 6, 112, COLS), BF16),
        pltpu.VMEM((2, GROUPS, CHIPS, 16, COLS), BF16),
        pltpu.VMEM((GROUPS, CHIPS, 16, COLS), BF16),
        pltpu.VMEM((GROUPS, CHIPS, 16, COLS), BF16),
        pltpu.VMEM((GROUPS, CHIPS, 16, COLS), BF16),
        pltpu.VMEM((128, COLS), F32),
        pltpu.VMEM((128, COLS), F32),
        pltpu.VMEM((GROUPS, 16, COLS), F32),
        pltpu.VMEM((GROUPS, 16, COLS), F32),
        pltpu.VMEM((CHIPS, 2, 16, COLS), BF16),
        pltpu.VMEM((CHIPS, 2, 16, COLS), BF16),
        pltpu.VMEM((GROUPS, 2, 16, COLS), F32),
        dma((2, 8)),
        dma((2, 8)),
        dma((2,)),
        dma((2,)),
        dma((GROUPS,)),
        dma((GROUPS,)),
        dma((GROUPS,)),
        dma((GROUPS,)),
        dma((CHIPS,)),
        dma((CHIPS,)),
        dma((GROUPS,)),
        dma((GROUPS,)),
    ]


def local(
    state_in,
    cotangent,
    ocean_mask,
    slot_column,
    dw_taps,
    dw_bias,
    norm_gain,
    norm_bias,
    up_weight,
    up_bias,
    down_weight,
    down_bias,
    layer_scale,
):
    vectors = jnp.stack([dw_bias, norm_gain, norm_bias, down_bias, layer_scale], axis=1)
    cols = jnp.concatenate([dw_taps, vectors], axis=1).astype(F32)
    up_wide = jnp.concatenate(
        [up_weight, up_bias[:, None], jnp.zeros((HIDDEN, PADDED - CHANNELS - 1), BF16)], axis=1
    )
    vmem = pl.BlockSpec(memory_space=pltpu.VMEM)
    grad_rows, tail = pl.pallas_call(
        kernel,
        out_shape=(
            jax.ShapeDtypeStruct((ROWS, CHANNELS, COLS), BF16),
            jax.ShapeDtypeStruct((GROUPS, 2, 16, COLS), F32),
        ),
        in_specs=[pl.BlockSpec(memory_space=pltpu.SMEM)] + [vmem] * 6,
        out_specs=(vmem, vmem),
        scratch_shapes=scratch(),
        compiler_params=pltpu.CompilerParams(
            collective_id=0, has_side_effects=True, vmem_limit_bytes=60 * 1024 * 1024
        ),
    )(slot_column, ocean_mask[0], state_in[0], cotangent[0], cols, up_wide, down_weight)
    grad_state = grad_rows.transpose(1, 0, 2)[None]
    weights = tail[:, 0].reshape(2, 4, 16, COLS).transpose(0, 2, 1, 3).reshape(32, 4 * COLS)
    grad_up = weights[:SHARE, :CHANNELS]
    grad_up_bias = weights[:SHARE, CHANNELS]
    grad_down = weights[:SHARE, 2 * COLS : 2 * COLS + CHANNELS].T
    small = tail[:, 1].reshape(128, COLS)
    wide = jnp.concatenate([small[:FOLD, :64], small[: CHANNELS - FOLD, 64:]], axis=0)
    return (
        grad_state,
        grad_up,
        grad_up_bias,
        grad_down,
        wide[:, :TAPS],
        wide[:, TAPS : TAPS + 5].T,
    )


def solution(mesh):
    slots = P(("group", "tile"), None, None, None)
    in_specs = (slots, slots, P(("group", "tile"), None, None), P(("group", "tile"))) + (P(),) * 9
    out_specs = (slots, P("tile", None), P("tile"), P(None, "tile"), P(), P())
    return jax.shard_map(local, mesh=mesh, in_specs=in_specs, out_specs=out_specs, check_vma=False)
```

```python
import math

import jax
import jax.numpy as jnp
from jax import lax
from jax.experimental import pallas as pl
from jax.experimental.pallas import tpu as pltpu
from jax.sharding import PartitionSpec as P

MESH = pl.DeviceIdType.MESH
F32 = jnp.float32
BF16 = jnp.bfloat16

CHANNELS = 200
PADDED = 208
HIDDEN = 800
KERNEL = 7
TAPS = KERNEL * KERNEL
MARGIN = 3
ROWS = 8
COLS = 128
CELLS = ROWS * COLS
TALL = ROWS + 2 * MARGIN
BLOCKS = CHANNELS // 8
FOLD = 104
GROUPS = 8
TILES = 32
CHIPS = TILES // 2
PLACES = 2 * GROUPS
SHARE = HIDDEN // TILES
CHUNK = 80
UNROLL = 5
VMEM_BYTES = 60 * 1024 * 1024

NORM_EPSILON = 1e-06
SQRT_HALF = 0.7071067811865476
GAUSS_SCALE = 0.3989422804014327

DW_BIAS, GAIN, SHIFT, DOWN_BIAS, SCALE = range(TAPS, TAPS + 5)


def shift_lanes(column):
    place = column if column < MARGIN else column - 1
    return slice(place * COLS, (place + 1) * COLS)


def moved_row(field, kept, row, rows, column):
    if column == MARGIN:
        return field[row, rows, :]
    return kept[row, rows, shift_lanes(column)]


INNER = tuple(range(MARGIN, MARGIN + ROWS))
OUTER = tuple(range(MARGIN)) + tuple(range(MARGIN + ROWS, TALL))


def convolve(field, kept, taps, rows, flipped, sources, total):
    for column in range(KERNEL):
        moved = {row: moved_row(field, kept, row, rows, column) for row in sources}
        for tap_row in range(KERNEL):
            reached = [row for row in range(ROWS) if row + tap_row in moved]
            if not reached:
                continue
            index = tap_row * KERNEL + column
            weight = taps[TAPS - 1 - index if flipped else index, rows, :]
            for row in reached:
                term = weight * moved[row + tap_row]
                total[row] = term if total[row] is None else total[row] + term
    return total


def block_rows(block):
    return pl.ds(pl.multiple_of(block * 8, 8), 8)


def lane_slice(row):
    return pl.ds(pl.multiple_of(row * COLS, COLS), COLS)


def iota(shape, dim):
    return lax.broadcasted_iota(jnp.int32, shape, dim)


def kernel(
    slot_ref,
    mask_ref,
    state_ref,
    cot_ref,
    taps_ref,
    upw_ref,
    downw_ref,
    bias_ref,
    gain_ref,
    shift_ref,
    dbias_ref,
    scale_ref,
    ubias_ref,
    gs_ref,
    tail_ref,
    mask_v,
    state_v,
    cot_v,
    taps_v,
    upw_v,
    downw_v,
    bias_v,
    gain_v,
    shift_v,
    dbias_v,
    scale_v,
    ubias_v,
    cols,
    moves,
    turns,
    flat,
    ext,
    exg,
    wide,
    taps,
    kept,
    normed,
    spread,
    mgrad,
    nlow,
    gblow,
    act,
    gpre,
    branch,
    gnorm,
    up_t,
    up_w,
    down_t,
    gup,
    gdown,
    sums,
    small_wide,
    gstate,
    rows_send,
    rows_recv,
    pack_send,
    pack_recv,
    w_send,
    w_core,
    w_group,
    w_group_in,
    w_tile,
    w_tile_in,
    w_final,
    small,
    small_in,
    s_tile,
    s_tile_in,
    s_final,
    load_sem,
    store_sem,
    halo_ssem,
    halo_rsem,
    core_ssem,
    core_rsem,
    wgroup_ssem,
    wgroup_rsem,
    small_ssem,
    small_rsem,
    wtile_ssem,
    wtile_rsem,
    stile_ssem,
    stile_rsem,
    wfinal_ssem,
    wfinal_rsem,
    sfinal_ssem,
    sfinal_rsem,
):
    g = lax.axis_index("group")
    t = lax.axis_index("tile")
    core = lax.rem(t, 2)
    chip = t // 2
    partner = chip * 2 + 1 - core
    place = g * 2 + core
    east = lax.rem(t + 1, TILES)
    west = lax.rem(t + TILES - 1, TILES)
    has_above = g > 0
    has_below = g < GROUPS - 1

    def remote(source, target, send, recv, gg, tt):
        return pltpu.make_async_remote_copy(
            src_ref=source,
            dst_ref=target,
            send_sem=send,
            recv_sem=recv,
            device_id=(gg, tt),
            device_id_type=MESH,
        )

    def finished(copy):
        copy.wait_send()
        copy.wait_recv()

    barrier = pltpu.get_barrier_semaphore()

    def greet(gg, tt):
        pl.semaphore_signal(barrier, inc=1, device_id=(gg, tt), device_id_type=MESH)

    def other_place(k):
        other = lax.rem(place + k, PLACES)
        return other // 2, chip * 2 + lax.rem(other, 2), other

    greet(g, east)
    greet(g, west)

    @pl.when(has_above)
    def _():
        greet(g - 1, east)
        greet(g - 1, west)

    @pl.when(has_below)
    def _():
        greet(g + 1, east)
        greet(g + 1, west)

    for k in range(1, PLACES):
        greet(*other_place(k)[:2])
    for k in range(1, CHIPS):
        greet(g, lax.rem(chip + k, CHIPS) * 2 + core)

    loads = [
        pltpu.make_async_copy(source, target, load_sem.at[index])
        for index, (source, target) in enumerate(
            [
                (state_ref, state_v),
                (mask_ref, mask_v),
                (taps_ref, taps_v),
                (bias_ref, bias_v),
                (gain_ref, gain_v),
                (shift_ref, shift_v),
                (dbias_ref, dbias_v),
                (scale_ref, scale_v),
                (cot_ref, cot_v),
                (upw_ref, upw_v),
                (ubias_ref, ubias_v),
                (downw_ref, downw_v),
            ]
        )
    ]
    for copy in loads:
        copy.start()

    def halo_copies(phase):
        def rows_copy(slot, gg):
            return remote(
                rows_send.at[phase, slot],
                rows_recv.at[phase, slot],
                halo_ssem.at[phase, slot],
                halo_rsem.at[phase, slot],
                gg,
                t,
            )

        def pack_copy(slot, gg, tt):
            return remote(
                pack_send.at[phase],
                pack_recv.at[phase, slot],
                halo_ssem.at[phase, 2 + slot],
                halo_rsem.at[phase, 2 + slot],
                gg,
                tt,
            )

        side = [pack_copy(0, g, west), pack_copy(1, g, east)]
        down = [rows_copy(0, g + 1), pack_copy(2, g + 1, west), pack_copy(3, g + 1, east)]
        up = [rows_copy(1, g - 1), pack_copy(4, g - 1, west), pack_copy(5, g - 1, east)]
        return side, down, up

    def halo_start(phase):
        side, down, up = halo_copies(phase)
        for copy in side:
            copy.start()

        @pl.when(has_below)
        def _():
            for copy in down:
                copy.start()

        @pl.when(has_above)
        def _():
            for copy in up:
                copy.start()

    def halo_wait_sides(phase):
        for copy in halo_copies(phase)[0]:
            finished(copy)

    def halo_wait_rest(phase):
        _, down, up = halo_copies(phase)

        @pl.when(has_below)
        def _():
            for copy in down:
                copy.wait_send()
            for copy in up:
                copy.wait_recv()

        @pl.when(has_above)
        def _():
            for copy in up:
                copy.wait_send()
            for copy in down:
                copy.wait_recv()

    def pack_up(phase, field):
        lane = iota((CHANNELS, COLS), 1)
        spot = lax.rem(lane + 3, COLS) // 8
        pack = field[MARGIN]
        for row in range(1, ROWS):
            pack = jnp.where(spot == row, pltpu.roll(field[MARGIN + row], 8 * row, 1), pack)
        second = pltpu.roll(pack[FOLD:], 64, 1)
        lane = iota((CHANNELS - FOLD, COLS), 1)
        first = jnp.where((lane >= 61) & (lane < 125), second, pack[: CHANNELS - FOLD])
        zeros = jnp.zeros((8, COLS), F32)
        whole = jnp.concatenate([first, pack[CHANNELS - FOLD : FOLD], zeros], axis=0)
        pack_send[phase] = whole.astype(BF16)
        pad = jnp.zeros((MARGIN, PADDED - CHANNELS, COLS), BF16)
        bottom = field[ROWS : ROWS + MARGIN].astype(BF16)
        top = field[MARGIN : 2 * MARGIN].astype(BF16)
        rows_send[phase, 0] = jnp.concatenate([bottom, pad], axis=1)
        rows_send[phase, 1] = jnp.concatenate([top, pad], axis=1)

    def unfold(phase, index):
        lane = iota((112, COLS), 1)
        from_east = pack_recv[phase, 2 * index].astype(F32)
        from_west = pack_recv[phase, 2 * index + 1].astype(F32)
        both = jnp.where(lax.rem(lane, 8) < 4, from_east, from_west)[:FOLD]
        return jnp.concatenate([both, pltpu.roll(both, 64, 1)], axis=0).astype(BF16)

    def move_inner(phase, field):
        for row in INNER:
            wide[row, :CHANNELS, :COLS] = field[row].astype(BF16)
        sides = jnp.dot(unfold(phase, 0), turns[...], preferred_element_type=F32).astype(BF16)
        for row in range(ROWS):
            wide[MARGIN + row, :, COLS:] = sides[:, row * COLS : (row + 1) * COLS]
        cells = wide[MARGIN : MARGIN + ROWS].reshape(ROWS * PADDED, 2 * COLS)
        out = jnp.dot(cells, moves[...], preferred_element_type=F32)
        kept[MARGIN : MARGIN + ROWS] = out.reshape(ROWS, PADDED, (KERNEL - 1) * COLS)

    def move_outer(phase, field):
        for index, first, begin in ((0, 0, ROWS - MARGIN), (1, MARGIN + ROWS, 0)):
            rows = rows_recv[phase, index]
            wide[first : first + MARGIN, :, :COLS] = rows
            field[first : first + MARGIN] = rows[:, :CHANNELS].astype(F32)
            turn = turns[:, begin * COLS : (begin + MARGIN) * COLS]
            sides = jnp.dot(unfold(phase, 1 + index), turn, preferred_element_type=F32)
            sides = sides.astype(BF16)
            for row in range(MARGIN):
                wide[first + row, :, COLS:] = sides[:, row * COLS : (row + 1) * COLS]
            cells = wide[first : first + MARGIN].reshape(MARGIN * PADDED, 2 * COLS)
            out = jnp.dot(cells, moves[...], preferred_element_type=F32)
            kept[first : first + MARGIN] = out.reshape(MARGIN, PADDED, (KERNEL - 1) * COLS)

    @pl.when(jnp.logical_not(has_above))
    def _():
        for phase in range(2):
            rows_recv[phase, 0] = jnp.zeros((MARGIN, PADDED, COLS), BF16)
            pack_recv[phase, 2] = jnp.zeros((112, COLS), BF16)
            pack_recv[phase, 3] = jnp.zeros((112, COLS), BF16)

    @pl.when(jnp.logical_not(has_below))
    def _():
        for phase in range(2):
            rows_recv[phase, 1] = jnp.zeros((MARGIN, PADDED, COLS), BF16)
            pack_recv[phase, 4] = jnp.zeros((112, COLS), BF16)
            pack_recv[phase, 5] = jnp.zeros((112, COLS), BF16)

    source = iota((2 * COLS, COLS), 0)
    lane = iota((2 * COLS, COLS), 1)
    for column in range(KERNEL):
        if column == MARGIN:
            continue
        wanted = lane + (column - MARGIN)
        beside = (wanted < 0) | (wanted >= COLS)
        wanted = jnp.where(beside, COLS + lax.rem(wanted + COLS, COLS), wanted)
        moves[:, shift_lanes(column)] = (source == wanted).astype(F32).astype(BF16)
    source = iota((COLS, COLS), 0)
    lane = iota((COLS, COLS), 1)
    edge = (lane < MARGIN) | (lane >= COLS - MARGIN)
    for row in range(ROWS):
        hit = edge & (source == lax.rem(lane + 8 * row, COLS))
        turns[:, row * COLS : (row + 1) * COLS] = hit.astype(F32).astype(BF16)

    live = (slot_ref[0] >= 0).astype(F32)
    loads[1].wait()
    loads[0].wait()
    mask = mask_v[...].astype(F32) * live
    flat[...] = (state_v[...].astype(F32) * mask[None]).reshape(CHANNELS * ROWS, COLS)
    for row in range(ROWS):
        ext[MARGIN + row] = flat[pl.ds(row, CHANNELS, stride=ROWS), :]
    pack_up(0, ext)

    for copy in loads[2:8]:
        copy.wait()
    vectors = [ref[...].astype(F32).reshape(1, CHANNELS) for ref in (bias_v, gain_v, shift_v, dbias_v, scale_v)]
    lines = [taps_v[...].astype(F32)] + vectors + [jnp.zeros((2, CHANNELS), F32)]
    cols[...] = jnp.concatenate(lines, axis=0).T
    for tap in range(TAPS):
        taps[tap] = jnp.broadcast_to(cols[:, tap : tap + 1], (CHANNELS, COLS))

    met = 2 + (PLACES - 1) + (CHIPS - 1)
    met = met + 2 * has_above.astype(jnp.int32) + 2 * has_below.astype(jnp.int32)
    pl.semaphore_wait(barrier, met)

    halo_start(0)
    loads[8].wait()
    flat[...] = (cot_v[...].astype(F32) * mask[None]).reshape(CHANNELS * ROWS, COLS)
    scale_col = cols[:, SCALE : SCALE + 1]
    for row in range(ROWS):
        masked = flat[pl.ds(row, CHANNELS, stride=ROWS), :]
        mgrad[row] = masked
        gblow[:, row * COLS : (row + 1) * COLS] = (masked * scale_col).astype(BF16)
    for copy in loads[9:]:
        copy.wait()
    bias_line = ubias_v[...].reshape(1, HIDDEN)
    below = jnp.where(iota((PADDED - CHANNELS, HIDDEN), 0) == 0, bias_line.astype(F32), 0.0)
    up_t[...] = jnp.concatenate([upw_v[...], below.astype(BF16)], axis=0)
    up_w[...] = up_t[...].T
    down_t[...] = downw_v[...].T

    halo_wait_sides(0)

    move_inner(0, ext)

    @pl.loop(0, BLOCKS, unroll=UNROLL)
    def _(block):
        rows = block_rows(block)
        total = convolve(ext, kept, taps, rows, False, INNER, [None] * ROWS)
        for row in range(ROWS):
            normed[row, rows, :] = total[row]

    halo_wait_rest(0)

    move_outer(0, ext)

    @pl.loop(0, BLOCKS, unroll=UNROLL)
    def _(block):
        rows = block_rows(block)
        total = [normed[row, rows, :] for row in range(ROWS)]
        total = convolve(ext, kept, taps, rows, False, OUTER, total)
        bias = cols[rows, DW_BIAS : DW_BIAS + 1]
        for row in range(ROWS):
            normed[row, rows, :] = (total[row] * live + bias).astype(BF16).astype(F32)

    gain_col = cols[:, GAIN : GAIN + 1]
    shift_col = cols[:, SHIFT : SHIFT + 1]

    @pl.loop(0, ROWS)
    def _(row):
        conv = normed[row]
        offset = conv - jnp.mean(conv, axis=0, keepdims=True)
        rate = lax.rsqrt(jnp.mean(offset * offset, axis=0, keepdims=True) + NORM_EPSILON)
        unit = offset * rate
        spread[row] = rate
        normed[row] = unit
        low = (unit * gain_col + shift_col).astype(BF16)
        tail = (iota((PADDED - CHANNELS, COLS), 0) == 0).astype(F32).astype(BF16)
        nlow[:, lane_slice(row)] = jnp.concatenate([low, tail], axis=0)

    @pl.loop(0, HIDDEN // CHUNK)
    def _(chunk):
        units = pl.ds(pl.multiple_of(chunk * CHUNK, CHUNK), CHUNK)
        pre = jnp.dot(up_w[units, :], nlow[...], preferred_element_type=F32)
        mass = 0.5 * (1.0 + lax.erf(pre * SQRT_HALF))
        density = GAUSS_SCALE * jnp.exp(-0.5 * pre * pre)
        act[units, :] = (pre * mass).astype(BF16)
        grad_act = jnp.dot(down_t[units, :], gblow[...], preferred_element_type=F32)
        gpre[units, :] = (grad_act * (mass + pre * density)).astype(BF16)

    branch[...] = jnp.dot(downw_v[...], act[...], preferred_element_type=F32)
    gnorm[...] = jnp.dot(up_t[...], gpre[...], preferred_element_type=F32)[:CHANNELS]

    sums[...] = jnp.zeros_like(sums)
    down_bias = cols[:, DOWN_BIAS : DOWN_BIAS + 1]

    @pl.loop(0, ROWS)
    def _(row):
        grad = gnorm[:, lane_slice(row)]
        unit = normed[row]
        masked = mgrad[row]
        sums[1] += grad * unit
        sums[2] += grad
        sums[3] += masked * scale_col
        sums[4] += masked * (branch[:, lane_slice(row)] + down_bias)
        scaled = grad * gain_col
        first = jnp.mean(scaled, axis=0, keepdims=True)
        second = jnp.mean(scaled * unit, axis=0, keepdims=True)
        low = (spread[row] * (scaled - first - unit * second)).astype(BF16).astype(F32)
        exg[MARGIN + row] = low
        sums[0] += low

    pack_up(1, exg)
    halo_start(1)

    trans = (((1,), (1,)), ((), ()))
    gup[:HIDDEN, :PADDED] = lax.dot_general(gpre[...], nlow[...], trans, preferred_element_type=F32)
    gdown[:HIDDEN, :CHANNELS] = lax.dot_general(
        act[...], gblow[...], trans, preferred_element_type=F32
    )

    for tile in range(TILES):
        for half in range(2):
            begin = tile * SHARE + 16 * half
            for part in range(4):
                source = gup if part < 2 else gdown
                side = (part % 2) * COLS
                piece = source[begin : begin + 16, side : side + COLS]
                if begin + 16 > HIDDEN:
                    piece = jnp.where(iota((16, COLS), 0) < HIDDEN - begin, piece, 0.0)
                w_send[tile % 2, half * 4 + part, tile // 2] = piece.astype(BF16)

    w_core_copy = remote(
        w_send.at[1 - core], w_core, core_ssem.at[0], core_rsem.at[0], g, partner
    )
    w_core_copy.start()

    def tap_block(block):
        rows = block_rows(block)
        lane = iota((8, COLS), 1)
        own = [exg[MARGIN + row, rows, :] for row in range(ROWS)]
        out = jnp.zeros((8, COLS), F32)
        for column in range(KERNEL):
            moved = [moved_row(ext, kept, row, rows, column) for row in range(TALL)]
            for tap_row in range(KERNEL):
                total = own[0] * moved[tap_row]
                for row in range(1, ROWS):
                    total = total + own[row] * moved[row + tap_row]
                spot = lane == tap_row * KERNEL + column
                out = jnp.where(spot, jnp.sum(total, axis=1, keepdims=True), out)
        for vector in range(5):
            total = jnp.sum(sums[vector, rows, :], axis=1, keepdims=True)
            out = jnp.where(lane == TAPS + vector, total, out)
        small_wide[rows, :] = out * live

    pl.loop(0, 10, unroll=UNROLL)(tap_block)

    finished(w_core_copy)

    @pl.loop(0, GROUPS)
    def _(piece):
        total = w_send[core, piece].astype(F32) + w_core[piece].astype(F32)
        w_group[piece] = total.astype(BF16)

    def w_group_copy(k):
        other = lax.rem(g + k, GROUPS)
        return remote(
            w_group.at[other], w_group_in.at[k], wgroup_ssem.at[k], wgroup_rsem.at[k], other, t
        )

    for k in range(1, GROUPS):
        w_group_copy(k).start()

    pl.loop(10, BLOCKS, unroll=UNROLL)(tap_block)

    second = pltpu.roll(small_wide[FOLD:], 64, 1)
    whole = jnp.concatenate(
        [
            small_wide[: CHANNELS - FOLD] + second,
            small_wide[CHANNELS - FOLD : FOLD],
            jnp.zeros((128 - FOLD, COLS), F32),
        ],
        axis=0,
    )
    small[...] = whole.reshape(PLACES, 8, COLS)

    def s_copy(k):
        gg, tt, other = other_place(k)
        return remote(small.at[other], small_in.at[k], small_ssem.at[k], small_rsem.at[k], gg, tt)

    for k in range(1, PLACES):
        s_copy(k).start()

    halo_wait_sides(1)

    move_inner(1, exg)

    def finish_inner(block):
        rows = block_rows(block)
        total = convolve(exg, kept, taps, rows, True, INNER, [None] * ROWS)
        for row in range(ROWS):
            gstate[row, rows, :] = total[row]

    def finish_outer(block):
        rows = block_rows(block)
        total = [gstate[row, rows, :] for row in range(ROWS)]
        total = convolve(exg, kept, taps, rows, True, OUTER, total)
        for row in range(ROWS):
            cell = mask[row : row + 1]
            spots = pl.ds(block * 64 + row, 8, stride=ROWS)
            flat[spots, :] = cell * (mgrad[row, rows, :] + total[row])

    pl.loop(0, 10, unroll=UNROLL)(finish_inner)

    total = w_group[g].astype(F32)
    for k in range(1, GROUPS):
        finished(w_group_copy(k))
        total = total + w_group_in[k].astype(F32)
    w_tile[...] = total.astype(BF16)

    def w_tile_copy(k):
        other = lax.rem(chip + k, CHIPS)
        return remote(
            w_tile.at[other],
            w_tile_in.at[chip],
            wtile_ssem.at[k],
            wtile_rsem.at[k],
            g,
            other * 2 + core,
        )

    for k in range(1, CHIPS):
        w_tile_copy(k).start()

    total = small[place]
    for k in range(1, PLACES):
        finished(s_copy(k))
        total = total + small_in[k]
    s_tile[...] = total

    def s_tile_copy(k):
        other = lax.rem(chip + k, CHIPS)
        return remote(
            s_tile, s_tile_in.at[chip], stile_ssem.at[k], stile_rsem.at[k], g, other * 2 + core
        )

    for k in range(1, CHIPS):
        s_tile_copy(k).start()

    pl.loop(10, BLOCKS, unroll=UNROLL)(finish_inner)

    halo_wait_rest(1)

    move_outer(1, exg)

    w_tile_in[chip] = w_tile[chip]
    for k in range(1, CHIPS):
        finished(w_tile_copy(k))
    total = w_tile_in[0].astype(F32)
    for other in range(1, CHIPS):
        total = total + w_tile_in[other].astype(F32)
    w_final[g] = total

    def w_final_copy(k):
        other = lax.rem(g + k, GROUPS)
        return remote(w_final.at[g], w_final.at[g], wfinal_ssem.at[k], wfinal_rsem.at[k], other, t)

    for k in range(1, GROUPS):
        w_final_copy(k).start()

    s_tile_in[chip] = s_tile[...]
    for k in range(1, CHIPS):
        finished(s_tile_copy(k))
    total = s_tile_in[0]
    for other in range(1, CHIPS):
        total = total + s_tile_in[other]
    s_final[place] = total

    def s_final_copy(k):
        gg, tt, _ = other_place(k)
        return remote(
            s_final.at[place], s_final.at[place], sfinal_ssem.at[k], sfinal_rsem.at[k], gg, tt
        )

    for k in range(1, PLACES):
        s_final_copy(k).start()

    pl.loop(0, BLOCKS, unroll=UNROLL)(finish_outer)

    state_v[...] = flat[...].reshape(CHANNELS, ROWS, COLS).astype(BF16)
    store = pltpu.make_async_copy(state_v, gs_ref, store_sem)
    store.start()

    for k in range(1, GROUPS):
        finished(w_final_copy(k))
    for k in range(1, PLACES):
        finished(s_final_copy(k))
    factor = 1.0 / math.sqrt(CELLS * GROUPS * TILES)
    tail_ref[0] = w_final[...].reshape(128, COLS) * factor
    tail_ref[1] = s_final[...].reshape(128, COLS) * factor
    store.wait()


def scratch():
    dma = pltpu.SemaphoreType.DMA
    tile = (CHANNELS, ROWS, COLS)
    rows = (ROWS, CHANNELS, COLS)
    tall = (TALL, CHANNELS, COLS)
    pieces = (GROUPS, CHIPS, 16, COLS)
    return [
        pltpu.VMEM((ROWS, COLS), jnp.int32),
        pltpu.VMEM(tile, BF16),
        pltpu.VMEM(tile, BF16),
        pltpu.VMEM((TAPS, CHANNELS), BF16),
        pltpu.VMEM((CHANNELS, HIDDEN), BF16),
        pltpu.VMEM((CHANNELS, HIDDEN), BF16),
        pltpu.VMEM((CHANNELS,), BF16),
        pltpu.VMEM((CHANNELS,), BF16),
        pltpu.VMEM((CHANNELS,), BF16),
        pltpu.VMEM((CHANNELS,), BF16),
        pltpu.VMEM((CHANNELS,), BF16),
        pltpu.VMEM((HIDDEN,), BF16),
        pltpu.VMEM((CHANNELS, 56), F32),
        pltpu.VMEM((2 * COLS, (KERNEL - 1) * COLS), BF16),
        pltpu.VMEM((COLS, ROWS * COLS), BF16),
        pltpu.VMEM((CHANNELS * ROWS, COLS), F32),
        pltpu.VMEM(tall, F32),
        pltpu.VMEM(tall, F32),
        pltpu.VMEM((TALL, PADDED, 2 * COLS), BF16),
        pltpu.VMEM((TAPS, CHANNELS, COLS), F32),
        pltpu.VMEM((TALL, PADDED, (KERNEL - 1) * COLS), F32),
        pltpu.VMEM(rows, F32),
        pltpu.VMEM((ROWS, 1, COLS), F32),
        pltpu.VMEM(rows, F32),
        pltpu.VMEM((PADDED, CELLS), BF16),
        pltpu.VMEM((CHANNELS, CELLS), BF16),
        pltpu.VMEM((HIDDEN, CELLS), BF16),
        pltpu.VMEM((HIDDEN, CELLS), BF16),
        pltpu.VMEM((CHANNELS, CELLS), F32),
        pltpu.VMEM((CHANNELS, CELLS), F32),
        pltpu.VMEM((PADDED, HIDDEN), BF16),
        pltpu.VMEM((HIDDEN, PADDED), BF16),
        pltpu.VMEM((HIDDEN, CHANNELS), BF16),
        pltpu.VMEM((HIDDEN + 8, 256), F32),
        pltpu.VMEM((HIDDEN + 8, 256), F32),
        pltpu.VMEM((5, CHANNELS, COLS), F32),
        pltpu.VMEM((CHANNELS, COLS), F32),
        pltpu.VMEM(rows, F32),
        pltpu.VMEM((2, 2, MARGIN, PADDED, COLS), BF16),
        pltpu.VMEM((2, 2, MARGIN, PADDED, COLS), BF16),
        pltpu.VMEM((2, 112, COLS), BF16),
        pltpu.VMEM((2, 6, 112, COLS), BF16),
        pltpu.VMEM((2,) + pieces, BF16),
        pltpu.VMEM(pieces, BF16),
        pltpu.VMEM(pieces, BF16),
        pltpu.VMEM(pieces, BF16),
        pltpu.VMEM((CHIPS, 16, COLS), BF16),
        pltpu.VMEM((CHIPS, 16, COLS), BF16),
        pltpu.VMEM((GROUPS, 16, COLS), F32),
        pltpu.VMEM((PLACES, 8, COLS), F32),
        pltpu.VMEM((PLACES, 8, COLS), F32),
        pltpu.VMEM((8, COLS), F32),
        pltpu.VMEM((CHIPS, 8, COLS), F32),
        pltpu.VMEM((PLACES, 8, COLS), F32),
        dma((12,)),
        dma(()),
        dma((2, 8)),
        dma((2, 8)),
        dma((1,)),
        dma((1,)),
        dma((GROUPS,)),
        dma((GROUPS,)),
        dma((PLACES,)),
        dma((PLACES,)),
        dma((CHIPS,)),
        dma((CHIPS,)),
        dma((CHIPS,)),
        dma((CHIPS,)),
        dma((GROUPS,)),
        dma((GROUPS,)),
        dma((PLACES,)),
        dma((PLACES,)),
    ]


def place_results(
    rows_ref, tail_ref, gs_ref, up_ref, ubias_ref, down_ref, taps_ref, vec_ref, rows, sems
):
    load = pltpu.make_async_copy(rows_ref, rows, sems.at[0])
    load.start()
    for half, size in ((0, 16), (1, SHARE - 16)):
        for part in range(4):
            piece = tail_ref[0, (half * 4 + part) * 16 : (half * 4 + part) * 16 + size, :]
            target = up_ref if part < 2 else down_ref
            begin = (part % 2) * COLS
            width = min(COLS, CHANNELS - begin)
            target[half * 16 : half * 16 + size, begin : begin + width] = piece[:, :width]
    load.wait()
    copy = pltpu.make_async_copy(rows, gs_ref, sems.at[1])
    copy.start()
    edge = jnp.concatenate([tail_ref[0, 16:32, :], tail_ref[0, 80:96, :]], axis=0)
    line = edge.T[CHANNELS - COLS : CHANNELS - COLS + 1, :SHARE]
    ubias_ref[...] = line.reshape(SHARE)
    turned = tail_ref[1].T
    low, high = turned[:64, :FOLD], turned[64:, : CHANNELS - FOLD]
    every = jnp.concatenate([low, high], axis=1)
    taps_ref[...] = every[:TAPS]
    vec_ref[...] = every[TAPS : TAPS + 5]
    copy.wait()


def local(
    state_in,
    cotangent,
    ocean_mask,
    slot_column,
    dw_taps,
    dw_bias,
    norm_gain,
    norm_bias,
    up_weight,
    up_bias,
    down_weight,
    down_bias,
    layer_scale,
):
    vmem = pl.BlockSpec(memory_space=pltpu.VMEM)
    anywhere = pl.BlockSpec(memory_space=pl.ANY)
    grad_rows, tail = pl.pallas_call(
        kernel,
        out_shape=(
            jax.ShapeDtypeStruct((CHANNELS, ROWS, COLS), BF16),
            jax.ShapeDtypeStruct((2, 128, COLS), F32),
        ),
        in_specs=[pl.BlockSpec(memory_space=pltpu.SMEM)] + [anywhere] * 12,
        out_specs=(anywhere, vmem),
        scratch_shapes=scratch(),
        compiler_params=pltpu.CompilerParams(
            collective_id=0, has_side_effects=True, vmem_limit_bytes=VMEM_BYTES
        ),
    )(
        slot_column,
        ocean_mask[0],
        state_in[0],
        cotangent[0],
        dw_taps.T,
        up_weight.T,
        down_weight,
        dw_bias,
        norm_gain,
        norm_bias,
        down_bias,
        layer_scale,
        up_bias,
    )
    grad_state, grad_up, grad_up_bias, grad_down, grad_taps, grad_vectors = pl.pallas_call(
        place_results,
        out_shape=(
            jax.ShapeDtypeStruct((CHANNELS, ROWS, COLS), BF16),
            jax.ShapeDtypeStruct((SHARE, CHANNELS), F32),
            jax.ShapeDtypeStruct((SHARE,), F32),
            jax.ShapeDtypeStruct((SHARE, CHANNELS), F32),
            jax.ShapeDtypeStruct((TAPS, CHANNELS), F32),
            jax.ShapeDtypeStruct((5, CHANNELS), F32),
        ),
        in_specs=[anywhere, vmem],
        out_specs=(anywhere,) + (vmem,) * 5,
        scratch_shapes=[pltpu.VMEM((CHANNELS, ROWS, COLS), BF16), pltpu.SemaphoreType.DMA((2,))],
    )(grad_rows, tail)
    return grad_state[None], grad_up, grad_up_bias, grad_down.T, grad_taps.T, grad_vectors


def solution(mesh):
    slots = P(("group", "tile"), None, None, None)
    in_specs = (slots, slots, P(("group", "tile"), None, None), P(("group", "tile"))) + (P(),) * 9
    out_specs = (slots, P("tile", None), P("tile"), P(None, "tile"), P(), P())
    return jax.shard_map(local, mesh=mesh, in_specs=in_specs, out_specs=out_specs, check_vma=False)
```

```python
import math

import jax
import jax.numpy as jnp
from jax import lax
from jax.experimental import pallas as pl
from jax.experimental.pallas import tpu as pltpu
from jax.sharding import PartitionSpec as P

MESH = pl.DeviceIdType.MESH
F32 = jnp.float32
BF16 = jnp.bfloat16

CHANNELS = 200
PADDED = 208
HIDDEN = 800
KERNEL = 7
TAPS = KERNEL * KERNEL
MARGIN = 3
ROWS = 8
COLS = 128
CELLS = ROWS * COLS
TALL = ROWS + 2 * MARGIN
BLOCKS = CHANNELS // 8
FOLD = 104
GROUPS = 8
DEPTH = 8
LINE = 4
TILES = 32
CHIPS = TILES // 2
PLANE = 2 * CHIPS
PLACES = 2 * GROUPS
SHARE = HIDDEN // TILES
CHUNK = 400
UNROLL = 5
VMEM_BYTES = 60 * 1024 * 1024

NORM_EPSILON = 1e-06
SQRT_HALF = 0.7071067811865476
GAUSS_SCALE = 0.3989422804014327

DW_BIAS, GAIN, SHIFT, DOWN_BIAS, SCALE = range(TAPS, TAPS + 5)


def shift_lanes(column):
    place = column if column < MARGIN else column - 1
    return slice(place * COLS, (place + 1) * COLS)


def moved_row(field, kept, row, rows, column):
    if column == MARGIN:
        return field[row, rows, :]
    return kept[row, rows, shift_lanes(column)]


INNER = tuple(range(MARGIN, MARGIN + ROWS))
OUTER = tuple(range(MARGIN)) + tuple(range(MARGIN + ROWS, TALL))


def convolve(field, kept, taps, rows, flipped, sources, total):
    for column in range(KERNEL):
        moved = {row: moved_row(field, kept, row, rows, column) for row in sources}
        for tap_row in range(KERNEL):
            reached = [row for row in range(ROWS) if row + tap_row in moved]
            if not reached:
                continue
            index = tap_row * KERNEL + column
            weight = taps[TAPS - 1 - index if flipped else index, rows, :]
            for row in reached:
                term = weight * moved[row + tap_row]
                total[row] = term if total[row] is None else total[row] + term
    return total


def block_rows(block):
    return pl.ds(pl.multiple_of(block * 8, 8), 8)


def lane_slice(row):
    return pl.ds(pl.multiple_of(row * COLS, COLS), COLS)


def iota(shape, dim):
    return lax.broadcasted_iota(jnp.int32, shape, dim)


def kernel(
    slot_ref,
    mask_ref,
    state_ref,
    cot_ref,
    taps_ref,
    upw_ref,
    downw_ref,
    bias_ref,
    gain_ref,
    shift_ref,
    dbias_ref,
    scale_ref,
    ubias_ref,
    gs_ref,
    tail_ref,
    mask_v,
    state_v,
    cot_v,
    taps_v,
    upw_v,
    downw_v,
    bias_v,
    gain_v,
    shift_v,
    dbias_v,
    scale_v,
    ubias_v,
    cols,
    moves,
    turns,
    flat,
    ext,
    exg,
    wide,
    taps,
    kept,
    normed,
    spread,
    mgrad,
    nlow,
    gblow,
    act,
    gpre,
    branch,
    gnorm,
    up_t,
    up_w,
    down_t,
    gup,
    gdown,
    sums,
    small_wide,
    gstate,
    rows_send,
    rows_recv,
    pack_send,
    pack_recv,
    w_send,
    w_core,
    w_group,
    w_group_in,
    w_tile,
    w_tile_in,
    w_final,
    small,
    small_in,
    s_tile,
    s_tile_in,
    s_final,
    load_sem,
    store_sem,
    halo_ssem,
    halo_rsem,
    core_ssem,
    core_rsem,
    wgroup_ssem,
    wgroup_rsem,
    small_ssem,
    small_rsem,
    wtile_ssem,
    wtile_rsem,
    stile_ssem,
    stile_rsem,
    wfinal_ssem,
    wfinal_rsem,
    sfinal_ssem,
    sfinal_rsem,
):
    g = lax.axis_index("group")
    t = lax.axis_index("tile")
    core = lax.rem(t, 2)
    chip = t // 2
    partner = chip * 2 + 1 - core
    place = g * 2 + core
    line = lax.rem(g, LINE)
    low = g // LINE
    plane = low * CHIPS + chip
    depth = chip // 2
    high = lax.rem(chip, 2)
    pillar = high * 2 + low
    sheet = line * DEPTH + depth
    upper = depth // 4
    east = lax.rem(t + 1, TILES)
    west = lax.rem(t + TILES - 1, TILES)
    has_above = g > 0
    has_below = g < GROUPS - 1

    def remote(source, target, send, recv, gg, tt):
        return pltpu.make_async_remote_copy(
            src_ref=source,
            dst_ref=target,
            send_sem=send,
            recv_sem=recv,
            device_id=(gg, tt),
            device_id_type=MESH,
        )

    def all_finished(buffer, count, send, recv):
        slots = buffer.at[pl.ds(0, count)]
        finished(remote(slots, slots, send, recv, g, partner))

    def finished(copy):
        copy.wait_send()
        copy.wait_recv()

    barrier = pltpu.get_barrier_semaphore()

    def greet(gg, tt):
        pl.semaphore_signal(barrier, inc=1, device_id=(gg, tt), device_id_type=MESH)

    def other_place(k):
        other = lax.rem(place + k, PLACES)
        return other // 2, chip * 2 + lax.rem(other, 2), other

    greet(g, east)
    greet(g, west)

    for k in range(1, PLACES):
        greet(*other_place(k)[:2])
    for k in range(1, CHIPS):
        other = lax.rem(chip + k, CHIPS) * 2 + core
        greet(g, other)
        greet(lax.rem(g + LINE, GROUPS), other)
    for k in range(1, LINE):
        for j in range(1, DEPTH):
            other = lax.rem(depth + j, DEPTH) * 2 + high
            greet(low * LINE + lax.rem(line + k, LINE), other * 2 + core)

    loads = [
        pltpu.make_async_copy(source, target, load_sem.at[index])
        for index, (source, target) in enumerate(
            [
                (state_ref, state_v),
                (mask_ref, mask_v),
                (taps_ref, taps_v),
                (bias_ref, bias_v),
                (gain_ref, gain_v),
                (shift_ref, shift_v),
                (dbias_ref, dbias_v),
                (scale_ref, scale_v),
                (cot_ref, cot_v),
                (upw_ref, upw_v),
                (ubias_ref, ubias_v),
                (downw_ref, downw_v),
            ]
        )
    ]
    for copy in loads:
        copy.start()

    def halo_copies(phase):
        def rows_copy(slot, gg):
            return remote(
                rows_send.at[phase, slot],
                rows_recv.at[phase, slot],
                halo_ssem.at[phase, slot],
                halo_rsem.at[phase, slot],
                gg,
                t,
            )

        def pack_copy(source, slot, gg, tt):
            return remote(
                pack_send.at[phase, source],
                pack_recv.at[phase, slot],
                halo_ssem.at[phase, 2 + slot],
                halo_rsem.at[phase, 2 + slot],
                gg,
                tt,
            )

        side = [pack_copy(0, 0, g, west), pack_copy(0, 1, g, east)]
        down = [rows_copy(0, g + 1), pack_copy(1, 2, g + 1, t)]
        up = [rows_copy(1, g - 1), pack_copy(1, 3, g - 1, t)]
        return side, down, up

    def halo_start_sides(phase):
        for copy in halo_copies(phase)[0]:
            copy.start()

    def halo_start_rest(phase, which):
        _, down, up = halo_copies(phase)

        @pl.when(has_below)
        def _():
            down[which].start()

        @pl.when(has_above)
        def _():
            up[which].start()

    def halo_wait_sides(phase):
        for copy in halo_copies(phase)[0]:
            finished(copy)

    def halo_wait_rest(phase):
        _, down, up = halo_copies(phase)

        @pl.when(has_below)
        def _():
            for copy in down:
                copy.wait_send()
            for copy in up:
                copy.wait_recv()

        @pl.when(has_above)
        def _():
            for copy in up:
                copy.wait_send()
            for copy in down:
                copy.wait_recv()

    def pack_up(phase, field):
        lane = iota((CHANNELS, COLS), 1)
        spot = lax.rem(lane + 3, COLS) // 8
        pack = field[MARGIN]
        for row in range(1, ROWS):
            pack = jnp.where(spot == row, pltpu.roll(field[MARGIN + row], 8 * row, 1), pack)
        second = pltpu.roll(pack[FOLD:], 64, 1)
        lane = iota((CHANNELS - FOLD, COLS), 1)
        first = jnp.where((lane >= 61) & (lane < 125), second, pack[: CHANNELS - FOLD])
        zeros = jnp.zeros((8, COLS), F32)
        whole = jnp.concatenate([first, pack[CHANNELS - FOLD : FOLD], zeros], axis=0)
        pack_send[phase, 0] = whole.astype(BF16)
        pad = jnp.zeros((MARGIN, PADDED - CHANNELS, COLS), BF16)
        bottom = field[ROWS : ROWS + MARGIN].astype(BF16)
        top = field[MARGIN : 2 * MARGIN].astype(BF16)
        rows_send[phase, 0] = jnp.concatenate([bottom, pad], axis=1)
        rows_send[phase, 1] = jnp.concatenate([top, pad], axis=1)

    def join_sides(phase):
        lane = iota((112, COLS), 1)
        from_east = pack_recv[phase, 0].astype(F32)
        from_west = pack_recv[phase, 1].astype(F32)
        both = jnp.where(lax.rem(lane, 8) < 4, from_east, from_west)
        pack_send[phase, 1] = both.astype(BF16)
        halo_start_rest(phase, 1)
        return both

    def unfold(both):
        first = both[:FOLD]
        return jnp.concatenate([first, pltpu.roll(first, 64, 1)], axis=0).astype(BF16)

    def move_inner(phase, field):
        for row in INNER:
            wide[row, :CHANNELS, :COLS] = field[row].astype(BF16)
        sides = jnp.dot(unfold(join_sides(phase)), turns[...], preferred_element_type=F32).astype(BF16)
        for row in range(ROWS):
            wide[MARGIN + row, :, COLS:] = sides[:, row * COLS : (row + 1) * COLS]
        cells = wide[MARGIN : MARGIN + ROWS].reshape(ROWS * PADDED, 2 * COLS)
        out = jnp.dot(cells, moves[...], preferred_element_type=F32)
        kept[MARGIN : MARGIN + ROWS] = out.reshape(ROWS, PADDED, (KERNEL - 1) * COLS)

    def move_outer(phase, field):
        for index, first, begin in ((0, 0, ROWS - MARGIN), (1, MARGIN + ROWS, 0)):
            rows = rows_recv[phase, index]
            wide[first : first + MARGIN, :, :COLS] = rows
            field[first : first + MARGIN] = rows[:, :CHANNELS].astype(F32)
            turn = turns[:, begin * COLS : (begin + MARGIN) * COLS]
            both = pack_recv[phase, 2 + index].astype(F32)
            sides = jnp.dot(unfold(both), turn, preferred_element_type=F32)
            sides = sides.astype(BF16)
            for row in range(MARGIN):
                wide[first + row, :, COLS:] = sides[:, row * COLS : (row + 1) * COLS]
            cells = wide[first : first + MARGIN].reshape(MARGIN * PADDED, 2 * COLS)
            out = jnp.dot(cells, moves[...], preferred_element_type=F32)
            kept[first : first + MARGIN] = out.reshape(MARGIN, PADDED, (KERNEL - 1) * COLS)

    @pl.when(jnp.logical_not(has_above))
    def _():
        for phase in range(2):
            rows_recv[phase, 0] = jnp.zeros((MARGIN, PADDED, COLS), BF16)
            pack_recv[phase, 2] = jnp.zeros((112, COLS), BF16)

    @pl.when(jnp.logical_not(has_below))
    def _():
        for phase in range(2):
            rows_recv[phase, 1] = jnp.zeros((MARGIN, PADDED, COLS), BF16)
            pack_recv[phase, 3] = jnp.zeros((112, COLS), BF16)

    source = iota((2 * COLS, COLS), 0)
    lane = iota((2 * COLS, COLS), 1)
    for column in range(KERNEL):
        if column == MARGIN:
            continue
        wanted = lane + (column - MARGIN)
        beside = (wanted < 0) | (wanted >= COLS)
        wanted = jnp.where(beside, COLS + lax.rem(wanted + COLS, COLS), wanted)
        moves[:, shift_lanes(column)] = (source == wanted).astype(F32).astype(BF16)
    source = iota((COLS, COLS), 0)
    lane = iota((COLS, COLS), 1)
    edge = (lane < MARGIN) | (lane >= COLS - MARGIN)
    for row in range(ROWS):
        hit = edge & (source == lax.rem(lane + 8 * row, COLS))
        turns[:, row * COLS : (row + 1) * COLS] = hit.astype(F32).astype(BF16)

    live = (slot_ref[0] >= 0).astype(F32)
    loads[1].wait()
    loads[0].wait()
    mask = mask_v[...].astype(F32) * live
    flat[...] = (state_v[...].astype(F32) * mask[None]).reshape(CHANNELS * ROWS, COLS)
    for row in range(ROWS):
        ext[MARGIN + row] = flat[pl.ds(row, CHANNELS, stride=ROWS), :]
    pack_up(0, ext)

    met = 2 + (PLACES - 1) + 2 * (CHIPS - 1) + (LINE - 1) * (DEPTH - 1)
    pl.semaphore_wait(barrier, met)

    halo_start_sides(0)
    for copy in loads[2:8]:
        copy.wait()
    vectors = [ref[...].astype(F32).reshape(1, CHANNELS) for ref in (bias_v, gain_v, shift_v, dbias_v, scale_v)]
    lines = [taps_v[...].astype(F32)] + vectors + [jnp.zeros((2, CHANNELS), F32)]
    cols[...] = jnp.concatenate(lines, axis=0).T
    for tap in range(TAPS):
        taps[tap] = jnp.broadcast_to(cols[:, tap : tap + 1], (CHANNELS, COLS))

    halo_start_rest(0, 0)
    loads[8].wait()
    flat[...] = (cot_v[...].astype(F32) * mask[None]).reshape(CHANNELS * ROWS, COLS)
    scale_col = cols[:, SCALE : SCALE + 1]
    for row in range(ROWS):
        masked = flat[pl.ds(row, CHANNELS, stride=ROWS), :]
        mgrad[row] = masked
        gblow[:, row * COLS : (row + 1) * COLS] = (masked * scale_col).astype(BF16)
    for copy in loads[9:]:
        copy.wait()
    bias_line = ubias_v[...].reshape(1, HIDDEN)
    below = jnp.where(iota((PADDED - CHANNELS, HIDDEN), 0) == 0, bias_line.astype(F32), 0.0)
    up_t[...] = jnp.concatenate([upw_v[...], below.astype(BF16)], axis=0)
    up_w[...] = up_t[...].T
    down_t[...] = downw_v[...].T

    halo_wait_sides(0)

    move_inner(0, ext)

    @pl.loop(0, BLOCKS, unroll=UNROLL)
    def _(block):
        rows = block_rows(block)
        total = convolve(ext, kept, taps, rows, False, INNER, [None] * ROWS)
        for row in range(ROWS):
            normed[row, rows, :] = total[row]

    halo_wait_rest(0)

    move_outer(0, ext)

    @pl.loop(0, BLOCKS, unroll=UNROLL)
    def _(block):
        rows = block_rows(block)
        total = [normed[row, rows, :] for row in range(ROWS)]
        total = convolve(ext, kept, taps, rows, False, OUTER, total)
        bias = cols[rows, DW_BIAS : DW_BIAS + 1]
        for row in range(ROWS):
            normed[row, rows, :] = (total[row] * live + bias).astype(BF16).astype(F32)

    gain_col = cols[:, GAIN : GAIN + 1]
    shift_col = cols[:, SHIFT : SHIFT + 1]

    @pl.loop(0, ROWS, unroll=ROWS)
    def _(row):
        conv = normed[row]
        offset = conv - jnp.mean(conv, axis=0, keepdims=True)
        rate = lax.rsqrt(jnp.mean(offset * offset, axis=0, keepdims=True) + NORM_EPSILON)
        unit = offset * rate
        spread[row] = rate
        normed[row] = unit
        low = (unit * gain_col + shift_col).astype(BF16)
        tail = (iota((PADDED - CHANNELS, COLS), 0) == 0).astype(F32).astype(BF16)
        nlow[:, lane_slice(row)] = jnp.concatenate([low, tail], axis=0)

    def w_core_copy(part):
        return remote(
            w_send.at[part, 1 - core],
            w_core.at[part],
            core_ssem.at[part],
            core_rsem.at[part],
            g,
            partner,
        )

    def w_line_copy(part, k):
        other = lax.rem((pillar if part == 0 else line) + k, LINE)
        if part == 0:
            gg, tt = lax.rem(other, 2) * LINE + line, (depth * 2 + other // 2) * 2 + core
        else:
            gg, tt = low * LINE + other, t
        return remote(
            w_group.at[part, other],
            w_group_in.at[part, k],
            wgroup_ssem.at[part],
            wgroup_rsem.at[part],
            gg,
            tt,
        )

    def mix(part):
        units = slice(part * CHUNK, (part + 1) * CHUNK)
        pre = jnp.dot(up_w[units, :], nlow[...], preferred_element_type=F32)
        mass = 0.5 * (1.0 + lax.erf(pre * SQRT_HALF))
        density = GAUSS_SCALE * jnp.exp(-0.5 * pre * pre)
        active = (pre * mass).astype(BF16)
        act[units, :] = active
        grad_act = jnp.dot(down_t[units, :], gblow[...], preferred_element_type=F32)
        grad_pre = (grad_act * (mass + pre * density)).astype(BF16)
        gpre[units, :] = grad_pre

    def weight_grads(part):
        units = slice(part * CHUNK, (part + 1) * CHUNK)
        trans = (((1,), (1,)), ((), ()))
        gup[units, :PADDED] = lax.dot_general(
            gpre[units, :], nlow[...], trans, preferred_element_type=F32
        )
        gdown[units, :CHANNELS] = lax.dot_general(
            act[units, :], gblow[...], trans, preferred_element_type=F32
        )
        for tile in range(part * TILES // 2, (part + 1) * TILES // 2):
            for half in range(2):
                begin = tile * SHARE + 16 * half
                for lanes in range(4):
                    source = gup if lanes < 2 else gdown
                    side = (lanes % 2) * COLS
                    piece = source[begin : begin + 16, side : side + COLS]
                    if begin + 16 > HIDDEN:
                        piece = jnp.where(iota((16, COLS), 0) < HIDDEN - begin, piece, 0.0)
                    along, across, spot = half * 2 + lanes // 2, lanes % 2, tile // 2
                    if part == 0:
                        first, second = spot % 2 * 2 + across, along * 4 + spot // 2
                    else:
                        first, second = along, across * 8 + spot - 8
                    w_send[part, tile % 2, first, second] = piece.astype(BF16)
        w_core_copy(part).start()

    def weight_share(part):
        finished(w_core_copy(part))

        @pl.loop(0, LINE)
        def _(piece):
            total = w_send[part, core, piece].astype(F32) + w_core[part, piece].astype(F32)
            w_group[part, piece] = total.astype(BF16)

        for k in range(1, LINE):
            w_line_copy(part, k).start()

    mix(0)

    weight_grads(0)

    mix(1)

    weight_grads(1)

    weight_share(0)

    branch[...] = jnp.dot(downw_v[...], act[...], preferred_element_type=F32)
    gnorm[...] = jnp.dot(up_t[...], gpre[...], preferred_element_type=F32)[:CHANNELS]

    weight_share(1)

    sums[...] = jnp.zeros_like(sums)
    down_bias = cols[:, DOWN_BIAS : DOWN_BIAS + 1]

    @pl.loop(0, ROWS, unroll=4)
    def _(row):
        grad = gnorm[:, lane_slice(row)]
        unit = normed[row]
        masked = mgrad[row]
        sums[1] += grad * unit
        sums[2] += grad
        sums[3] += masked * scale_col
        sums[4] += masked * (branch[:, lane_slice(row)] + down_bias)
        scaled = grad * gain_col
        first = jnp.mean(scaled, axis=0, keepdims=True)
        second = jnp.mean(scaled * unit, axis=0, keepdims=True)
        low = (spread[row] * (scaled - first - unit * second)).astype(BF16).astype(F32)
        exg[MARGIN + row] = low
        sums[0] += low

    pack_up(1, exg)
    halo_start_sides(1)
    halo_start_rest(1, 0)

    def tap_block(block):
        rows = block_rows(block)
        lane = iota((8, COLS), 1)
        own = [exg[MARGIN + row, rows, :] for row in range(ROWS)]
        out = jnp.zeros((8, COLS), F32)
        for column in range(KERNEL):
            moved = [moved_row(ext, kept, row, rows, column) for row in range(TALL)]
            for tap_row in range(KERNEL):
                total = own[0] * moved[tap_row]
                for row in range(1, ROWS):
                    total = total + own[row] * moved[row + tap_row]
                spot = lane == tap_row * KERNEL + column
                out = jnp.where(spot, jnp.sum(total, axis=1, keepdims=True), out)
        for vector in range(5):
            total = jnp.sum(sums[vector, rows, :], axis=1, keepdims=True)
            out = jnp.where(lane == TAPS + vector, total, out)
        small_wide[rows, :] = out * live

    pl.loop(0, BLOCKS, unroll=UNROLL)(tap_block)

    second = pltpu.roll(small_wide[FOLD:], 64, 1)
    whole = jnp.concatenate(
        [
            small_wide[: CHANNELS - FOLD] + second,
            small_wide[CHANNELS - FOLD : FOLD],
            jnp.zeros((128 - FOLD, COLS), F32),
        ],
        axis=0,
    )
    small[...] = whole.reshape(PLACES, 8, COLS)

    def s_copy(k):
        gg, tt, other = other_place(k)
        return remote(small.at[other], small_in.at[k], small_ssem, small_rsem, gg, tt)

    for k in range(1, PLACES):
        s_copy(k).start()

    halo_wait_sides(1)

    move_inner(1, exg)

    def finish_inner(block):
        rows = block_rows(block)
        total = convolve(exg, kept, taps, rows, True, INNER, [None] * ROWS)
        for row in range(ROWS):
            gstate[row, rows, :] = total[row]

    def finish_outer(block):
        rows = block_rows(block)
        total = [gstate[row, rows, :] for row in range(ROWS)]
        total = convolve(exg, kept, taps, rows, True, OUTER, total)
        for row in range(ROWS):
            cell = mask[row : row + 1]
            spots = pl.ds(block * 64 + row, 8, stride=ROWS)
            flat[spots, :] = cell * (mgrad[row, rows, :] + total[row])

    pl.loop(0, 15, unroll=UNROLL)(finish_inner)

    for part in range(2):
        total = w_group[part, pillar if part == 0 else line].astype(F32)
        all_finished(w_group_in.at[part], LINE - 1, wgroup_ssem.at[part], wgroup_rsem.at[part])
        for k in range(1, LINE):
            total = total + w_group_in[part, k].astype(F32)
        w_tile[part] = total.astype(BF16)

    near = line * 4 + lax.rem(depth, 4)
    far = low * 8 + lax.rem(chip, 8)

    def w_tile_copy(part, k):
        if part == 0:
            other = lax.rem(near + k, 16)
            gg, tt = low * LINE + other // 4, (lax.rem(other, 4) * 2 + high) * 2 + core
        else:
            other = lax.rem(far + k, 16)
            gg, tt = other // 8 * LINE + line, (8 + lax.rem(other, 8)) * 2 + core
        return remote(
            w_tile.at[part, other],
            w_tile_in.at[sheet if part == 0 else plane],
            wtile_ssem,
            wtile_rsem,
            gg,
            tt,
        )

    for k in range(1, 16):
        w_tile_copy(0, k).start()
        w_tile_copy(1, k).start()

    @pl.when(upper == 1)
    def _():
        w_tile_copy(0, 0).start()

    @pl.when(upper == 0)
    def _():
        w_tile_copy(1, 0).start()

    total = small[place]
    all_finished(small_in, PLACES - 1, small_ssem, small_rsem)
    for k in range(1, PLACES):
        total = total + small_in[k]
    s_tile[...] = total

    def s_tile_copy(k):
        other = lax.rem(chip + k, CHIPS)
        return remote(
            s_tile, s_tile_in.at[chip], stile_ssem, stile_rsem, g, other * 2 + core
        )

    for k in range(1, CHIPS):
        s_tile_copy(k).start()

    pl.loop(15, BLOCKS, unroll=UNROLL)(finish_inner)

    halo_wait_rest(1)

    move_outer(1, exg)

    pl.loop(0, BLOCKS, unroll=UNROLL)(finish_outer)

    state_v[...] = flat[...].reshape(CHANNELS, ROWS, COLS).astype(BF16)
    store = pltpu.make_async_copy(state_v, gs_ref, store_sem)
    store.start()

    w_tile_in[upper * plane + (1 - upper) * sheet] = w_tile[upper, upper * far + (1 - upper) * near]
    all_finished(w_tile_in, PLANE - 1, wtile_ssem, wtile_rsem)
    total = w_tile_in[0].astype(F32)
    for other in range(1, PLANE):
        total = total + w_tile_in[other].astype(F32)
    piece = line * 2 + low
    w_final[piece] = total

    def w_final_copy(k):
        other = lax.rem(g + k, GROUPS)
        return remote(
            w_final.at[piece], w_final.at[piece], wfinal_ssem, wfinal_rsem, other, t
        )

    for k in range(1, GROUPS):
        w_final_copy(k).start()

    s_tile_in[chip] = s_tile[...]
    all_finished(s_tile_in, CHIPS - 1, stile_ssem, stile_rsem)
    total = s_tile_in[0]
    for other in range(1, CHIPS):
        total = total + s_tile_in[other]
    s_final[place] = total

    def s_final_copy(k):
        gg, tt, _ = other_place(k)
        return remote(
            s_final.at[place], s_final.at[place], sfinal_ssem, sfinal_rsem, gg, tt
        )

    for k in range(1, PLACES):
        s_final_copy(k).start()

    all_finished(w_final, GROUPS - 1, wfinal_ssem, wfinal_rsem)
    all_finished(s_final, PLACES - 1, sfinal_ssem, sfinal_rsem)
    factor = 1.0 / math.sqrt(CELLS * GROUPS * TILES)
    tail_ref[0] = w_final[...].reshape(128, COLS) * factor
    tail_ref[1] = s_final[...].reshape(128, COLS) * factor
    store.wait()


def scratch():
    dma = pltpu.SemaphoreType.DMA
    tile = (CHANNELS, ROWS, COLS)
    rows = (ROWS, CHANNELS, COLS)
    tall = (TALL, CHANNELS, COLS)
    pieces = (LINE, 16, 16, COLS)
    return [
        pltpu.VMEM((ROWS, COLS), jnp.int32),
        pltpu.VMEM(tile, BF16),
        pltpu.VMEM(tile, BF16),
        pltpu.VMEM((TAPS, CHANNELS), BF16),
        pltpu.VMEM((CHANNELS, HIDDEN), BF16),
        pltpu.VMEM((CHANNELS, HIDDEN), BF16),
        pltpu.VMEM((CHANNELS,), BF16),
        pltpu.VMEM((CHANNELS,), BF16),
        pltpu.VMEM((CHANNELS,), BF16),
        pltpu.VMEM((CHANNELS,), BF16),
        pltpu.VMEM((CHANNELS,), BF16),
        pltpu.VMEM((HIDDEN,), BF16),
        pltpu.VMEM((CHANNELS, 56), F32),
        pltpu.VMEM((2 * COLS, (KERNEL - 1) * COLS), BF16),
        pltpu.VMEM((COLS, ROWS * COLS), BF16),
        pltpu.VMEM((CHANNELS * ROWS, COLS), F32),
        pltpu.VMEM(tall, F32),
        pltpu.VMEM(tall, F32),
        pltpu.VMEM((TALL, PADDED, 2 * COLS), BF16),
        pltpu.VMEM((TAPS, CHANNELS, COLS), F32),
        pltpu.VMEM((TALL, PADDED, (KERNEL - 1) * COLS), F32),
        pltpu.VMEM(rows, F32),
        pltpu.VMEM((ROWS, 1, COLS), F32),
        pltpu.VMEM(rows, F32),
        pltpu.VMEM((PADDED, CELLS), BF16),
        pltpu.VMEM((CHANNELS, CELLS), BF16),
        pltpu.VMEM((HIDDEN, CELLS), BF16),
        pltpu.VMEM((HIDDEN, CELLS), BF16),
        pltpu.VMEM((CHANNELS, CELLS), F32),
        pltpu.VMEM((CHANNELS, CELLS), F32),
        pltpu.VMEM((PADDED, HIDDEN), BF16),
        pltpu.VMEM((HIDDEN, PADDED), BF16),
        pltpu.VMEM((HIDDEN, CHANNELS), BF16),
        pltpu.VMEM((HIDDEN + 8, 256), F32),
        pltpu.VMEM((HIDDEN + 8, 256), F32),
        pltpu.VMEM((5, CHANNELS, COLS), F32),
        pltpu.VMEM((CHANNELS, COLS), F32),
        pltpu.VMEM(rows, F32),
        pltpu.VMEM((2, 2, MARGIN, PADDED, COLS), BF16),
        pltpu.VMEM((2, 2, MARGIN, PADDED, COLS), BF16),
        pltpu.VMEM((2, 2, 112, COLS), BF16),
        pltpu.VMEM((2, 4, 112, COLS), BF16),
        pltpu.VMEM((2, 2) + pieces, BF16),
        pltpu.VMEM((2,) + pieces, BF16),
        pltpu.VMEM((2,) + pieces, BF16),
        pltpu.VMEM((2,) + pieces, BF16),
        pltpu.VMEM((2, 16, 16, COLS), BF16),
        pltpu.VMEM((PLANE, 16, COLS), BF16),
        pltpu.VMEM((GROUPS, 16, COLS), F32),
        pltpu.VMEM((PLACES, 8, COLS), F32),
        pltpu.VMEM((PLACES, 8, COLS), F32),
        pltpu.VMEM((8, COLS), F32),
        pltpu.VMEM((CHIPS, 8, COLS), F32),
        pltpu.VMEM((PLACES, 8, COLS), F32),
        dma((12,)),
        dma(()),
        dma((2, 6)),
        dma((2, 6)),
        dma((2,)),
        dma((2,)),
        dma((2,)),
        dma((2,)),
        dma(()),
        dma(()),
        dma(()),
        dma(()),
        dma(()),
        dma(()),
        dma(()),
        dma(()),
        dma(()),
        dma(()),
    ]


def place_results(rows_ref, tail_ref, gs_ref, up_ref, ubias_ref, down_ref, taps_ref, vec_ref, sem):
    copy = pltpu.make_async_copy(rows_ref, gs_ref, sem)
    copy.start()
    for half, size in ((0, 16), (1, SHARE - 16)):
        for part in range(4):
            piece = tail_ref[0, (half * 4 + part) * 16 : (half * 4 + part) * 16 + size, :]
            target = up_ref if part < 2 else down_ref
            begin = (part % 2) * COLS
            width = min(COLS, CHANNELS - begin)
            target[half * 16 : half * 16 + size, begin : begin + width] = piece[:, :width]
    edge = jnp.concatenate([tail_ref[0, 16:32, :], tail_ref[0, 80:96, :]], axis=0)
    line = edge.T[CHANNELS - COLS : CHANNELS - COLS + 1, :SHARE]
    ubias_ref[...] = line.reshape(SHARE)
    turned = tail_ref[1].T
    low, high = turned[:64, :FOLD], turned[64:, : CHANNELS - FOLD]
    every = jnp.concatenate([low, high], axis=1)
    taps_ref[...] = every[:TAPS]
    vec_ref[...] = every[TAPS : TAPS + 5]
    copy.wait()


def local(
    state_in,
    cotangent,
    ocean_mask,
    slot_column,
    dw_taps,
    dw_bias,
    norm_gain,
    norm_bias,
    up_weight,
    up_bias,
    down_weight,
    down_bias,
    layer_scale,
):
    vmem = pl.BlockSpec(memory_space=pltpu.VMEM)
    anywhere = pl.BlockSpec(memory_space=pl.ANY)
    grad_rows, tail = pl.pallas_call(
        kernel,
        out_shape=(
            jax.ShapeDtypeStruct((CHANNELS, ROWS, COLS), BF16),
            jax.ShapeDtypeStruct((2, 128, COLS), F32),
        ),
        in_specs=[pl.BlockSpec(memory_space=pltpu.SMEM)] + [anywhere] * 12,
        out_specs=(anywhere, vmem),
        scratch_shapes=scratch(),
        compiler_params=pltpu.CompilerParams(
            collective_id=0, has_side_effects=True, vmem_limit_bytes=VMEM_BYTES
        ),
    )(
        slot_column,
        ocean_mask[0],
        state_in[0],
        cotangent[0],
        dw_taps.T,
        up_weight.T,
        down_weight,
        dw_bias,
        norm_gain,
        norm_bias,
        down_bias,
        layer_scale,
        up_bias,
    )
    grad_state, grad_up, grad_up_bias, grad_down, grad_taps, grad_vectors = pl.pallas_call(
        place_results,
        out_shape=(
            jax.ShapeDtypeStruct((CHANNELS, ROWS, COLS), BF16),
            jax.ShapeDtypeStruct((SHARE, CHANNELS), F32),
            jax.ShapeDtypeStruct((SHARE,), F32),
            jax.ShapeDtypeStruct((SHARE, CHANNELS), F32),
            jax.ShapeDtypeStruct((TAPS, CHANNELS), F32),
            jax.ShapeDtypeStruct((5, CHANNELS), F32),
        ),
        in_specs=[vmem, vmem],
        out_specs=(anywhere,) + (vmem,) * 5,
        scratch_shapes=[pltpu.SemaphoreType.DMA(())],
    )(grad_rows, tail)
    return grad_state[None], grad_up, grad_up_bias, grad_down.T, grad_taps.T, grad_vectors


def solution(mesh):
    slots = P(("group", "tile"), None, None, None)
    in_specs = (slots, slots, P(("group", "tile"), None, None), P(("group", "tile"))) + (P(),) * 9
    out_specs = (slots, P("tile", None), P("tile"), P(None, "tile"), P(), P())
    return jax.shard_map(local, mesh=mesh, in_specs=in_specs, out_specs=out_specs, check_vma=False)
```

```python
import math

import jax
import jax.numpy as jnp
from jax import lax
from jax.experimental import pallas as pl
from jax.experimental.pallas import tpu as pltpu
from jax.sharding import PartitionSpec as P

MESH = pl.DeviceIdType.MESH
F32 = jnp.float32
BF16 = jnp.bfloat16

CHANNELS = 200
PADDED = 208
HIDDEN = 800
KERNEL = 7
TAPS = KERNEL * KERNEL
MARGIN = 3
ROWS = 8
COLS = 128
CELLS = ROWS * COLS
TALL = ROWS + 2 * MARGIN
BLOCKS = CHANNELS // 8
FOLD = 104
GROUPS = 8
DEPTH = 8
LINE = 4
TILES = 32
CHIPS = TILES // 2
PLANE = 2 * CHIPS
PLACES = 2 * GROUPS
SHARE = HIDDEN // TILES
CHUNK = 400
UNROLL = 5
VMEM_BYTES = 60 * 1024 * 1024

NORM_EPSILON = 1e-06
SQRT_HALF = 0.7071067811865476
GAUSS_SCALE = 0.3989422804014327

DW_BIAS, GAIN, SHIFT, DOWN_BIAS, SCALE = range(TAPS, TAPS + 5)


def shift_lanes(column):
    place = column if column < MARGIN else column - 1
    return slice(place * COLS, (place + 1) * COLS)


def moved_row(field, kept, row, rows, column):
    if column == MARGIN:
        return field[row, rows, :]
    return kept[row, rows, shift_lanes(column)]


INNER = tuple(range(MARGIN, MARGIN + ROWS))
OUTER = tuple(range(MARGIN)) + tuple(range(MARGIN + ROWS, TALL))


def convolve(field, kept, taps, rows, flipped, sources, total):
    for column in range(KERNEL):
        moved = {row: moved_row(field, kept, row, rows, column) for row in sources}
        for tap_row in range(KERNEL):
            reached = [row for row in range(ROWS) if row + tap_row in moved]
            if not reached:
                continue
            index = tap_row * KERNEL + column
            weight = taps[TAPS - 1 - index if flipped else index, rows, :]
            for row in reached:
                term = weight * moved[row + tap_row]
                total[row] = term if total[row] is None else total[row] + term
    return total


def block_rows(block):
    return pl.ds(pl.multiple_of(block * 8, 8), 8)


def lane_slice(row):
    return pl.ds(pl.multiple_of(row * COLS, COLS), COLS)


def iota(shape, dim):
    return lax.broadcasted_iota(jnp.int32, shape, dim)


def kernel(
    slot_ref,
    mask_ref,
    state_ref,
    cot_ref,
    taps_ref,
    upw_ref,
    downw_ref,
    bias_ref,
    gain_ref,
    shift_ref,
    dbias_ref,
    scale_ref,
    ubias_ref,
    gs_ref,
    tail_ref,
    mask_v,
    state_v,
    cot_v,
    taps_v,
    upw_v,
    downw_v,
    bias_v,
    gain_v,
    shift_v,
    dbias_v,
    scale_v,
    ubias_v,
    cols,
    moves,
    turns,
    flat,
    ext,
    exg,
    wide,
    taps,
    kept,
    normed,
    spread,
    mgrad,
    nlow,
    gblow,
    act,
    gpre,
    branch,
    gnorm,
    up_t,
    up_w,
    down_t,
    gup,
    gdown,
    sums,
    small_wide,
    gstate,
    rows_send,
    rows_recv,
    pack_send,
    pack_recv,
    w_send,
    w_core,
    w_group,
    w_group_in,
    w_tile,
    w_tile_in,
    w_final,
    small,
    small_in,
    s_tile,
    s_tile_in,
    s_final,
    load_sem,
    store_sem,
    halo_ssem,
    halo_rsem,
    core_ssem,
    core_rsem,
    wgroup_ssem,
    wgroup_rsem,
    small_ssem,
    small_rsem,
    wtile_ssem,
    wtile_rsem,
    stile_ssem,
    stile_rsem,
    wfinal_ssem,
    wfinal_rsem,
    sfinal_ssem,
    sfinal_rsem,
):
    g = lax.axis_index("group")
    t = lax.axis_index("tile")
    core = lax.rem(t, 2)
    chip = t // 2
    partner = chip * 2 + 1 - core
    place = g * 2 + core
    line = lax.rem(g, LINE)
    low = g // LINE
    plane = low * CHIPS + chip
    depth = chip // 2
    high = lax.rem(chip, 2)
    pillar = high * 2 + low
    sheet = line * DEPTH + depth
    upper = depth // 4
    east = lax.rem(t + 1, TILES)
    west = lax.rem(t + TILES - 1, TILES)
    has_above = g > 0
    has_below = g < GROUPS - 1

    def remote(source, target, send, recv, gg, tt):
        return pltpu.make_async_remote_copy(
            src_ref=source,
            dst_ref=target,
            send_sem=send,
            recv_sem=recv,
            device_id=(gg, tt),
            device_id_type=MESH,
        )

    def all_finished(buffer, count, send, recv):
        slots = buffer.at[pl.ds(0, count)]
        finished(remote(slots, slots, send, recv, g, partner))

    def finished(copy):
        copy.wait_send()
        copy.wait_recv()

    barrier = pltpu.get_barrier_semaphore()

    def greet(gg, tt):
        pl.semaphore_signal(barrier, inc=1, device_id=(gg, tt), device_id_type=MESH)

    def other_place(k):
        other = lax.rem(place + k, PLACES)
        return other // 2, chip * 2 + lax.rem(other, 2), other

    greet(g, east)
    greet(g, west)

    for k in range(1, PLACES):
        greet(*other_place(k)[:2])
    for k in range(1, CHIPS):
        other = lax.rem(chip + k, CHIPS) * 2 + core
        greet(g, other)
        greet(lax.rem(g + LINE, GROUPS), other)
    for k in range(1, LINE):
        for j in range(1, DEPTH):
            other = lax.rem(depth + j, DEPTH) * 2 + high
            greet(low * LINE + lax.rem(line + k, LINE), other * 2 + core)

    loads = [
        pltpu.make_async_copy(source, target, load_sem.at[index])
        for index, (source, target) in enumerate(
            [
                (state_ref, state_v),
                (mask_ref, mask_v),
                (taps_ref, taps_v),
                (bias_ref, bias_v),
                (gain_ref, gain_v),
                (shift_ref, shift_v),
                (dbias_ref, dbias_v),
                (scale_ref, scale_v),
                (cot_ref, cot_v),
                (upw_ref, upw_v),
                (ubias_ref, ubias_v),
                (downw_ref, downw_v),
            ]
        )
    ]
    for copy in loads:
        copy.start()

    def halo_copies(phase):
        def rows_copy(slot, gg):
            return remote(
                rows_send.at[phase, slot],
                rows_recv.at[phase, slot],
                halo_ssem.at[phase, slot],
                halo_rsem.at[phase, slot],
                gg,
                t,
            )

        def pack_copy(source, slot, gg, tt):
            return remote(
                pack_send.at[phase, source],
                pack_recv.at[phase, slot],
                halo_ssem.at[phase, 2 + slot],
                halo_rsem.at[phase, 2 + slot],
                gg,
                tt,
            )

        side = [pack_copy(0, 0, g, west), pack_copy(0, 1, g, east)]
        down = [rows_copy(0, g + 1), pack_copy(1, 2, g + 1, t)]
        up = [rows_copy(1, g - 1), pack_copy(1, 3, g - 1, t)]
        return side, down, up

    def halo_start_sides(phase):
        for copy in halo_copies(phase)[0]:
            copy.start()

    def halo_start_rest(phase, which):
        _, down, up = halo_copies(phase)

        @pl.when(has_below)
        def _():
            down[which].start()

        @pl.when(has_above)
        def _():
            up[which].start()

    def halo_wait_sides(phase):
        for copy in halo_copies(phase)[0]:
            finished(copy)

    def halo_wait_rest(phase):
        _, down, up = halo_copies(phase)

        @pl.when(has_below)
        def _():
            for copy in down:
                copy.wait_send()
            for copy in up:
                copy.wait_recv()

        @pl.when(has_above)
        def _():
            for copy in up:
                copy.wait_send()
            for copy in down:
                copy.wait_recv()

    def pack_up(phase, field):
        lane = iota((CHANNELS, COLS), 1)
        spot = lax.rem(lane + 3, COLS) // 8
        pack = field[MARGIN]
        for row in range(1, ROWS):
            pack = jnp.where(spot == row, pltpu.roll(field[MARGIN + row], 8 * row, 1), pack)
        second = pltpu.roll(pack[FOLD:], 64, 1)
        lane = iota((CHANNELS - FOLD, COLS), 1)
        first = jnp.where((lane >= 61) & (lane < 125), second, pack[: CHANNELS - FOLD])
        zeros = jnp.zeros((8, COLS), F32)
        whole = jnp.concatenate([first, pack[CHANNELS - FOLD : FOLD], zeros], axis=0)
        pack_send[phase, 0] = whole.astype(BF16)
        pad = jnp.zeros((MARGIN, PADDED - CHANNELS, COLS), BF16)
        bottom = field[ROWS : ROWS + MARGIN].astype(BF16)
        top = field[MARGIN : 2 * MARGIN].astype(BF16)
        rows_send[phase, 0] = jnp.concatenate([bottom, pad], axis=1)
        rows_send[phase, 1] = jnp.concatenate([top, pad], axis=1)

    def join_sides(phase):
        lane = iota((112, COLS), 1)
        from_east = pack_recv[phase, 0].astype(F32)
        from_west = pack_recv[phase, 1].astype(F32)
        both = jnp.where(lax.rem(lane, 8) < 4, from_east, from_west)
        pack_send[phase, 1] = both.astype(BF16)
        halo_start_rest(phase, 1)
        return both

    def unfold(both):
        first = both[:FOLD]
        return jnp.concatenate([first, pltpu.roll(first, 64, 1)], axis=0).astype(BF16)

    def fill_inner(field):
        for row in INNER:
            wide[row, :CHANNELS, :COLS] = field[row].astype(BF16)

    def move_inner(phase):
        sides = jnp.dot(unfold(join_sides(phase)), turns[...], preferred_element_type=F32).astype(BF16)
        for row in range(ROWS):
            wide[MARGIN + row, :, COLS:] = sides[:, row * COLS : (row + 1) * COLS]
        cells = wide[MARGIN : MARGIN + ROWS].reshape(ROWS * PADDED, 2 * COLS)
        out = jnp.dot(cells, moves[...], preferred_element_type=F32)
        kept[MARGIN : MARGIN + ROWS] = out.reshape(ROWS, PADDED, (KERNEL - 1) * COLS)

    def move_outer(phase, field):
        for index, first, begin in ((0, 0, ROWS - MARGIN), (1, MARGIN + ROWS, 0)):
            rows = rows_recv[phase, index]
            wide[first : first + MARGIN, :, :COLS] = rows
            field[first : first + MARGIN] = rows[:, :CHANNELS].astype(F32)
            turn = turns[:, begin * COLS : (begin + MARGIN) * COLS]
            both = pack_recv[phase, 2 + index].astype(F32)
            sides = jnp.dot(unfold(both), turn, preferred_element_type=F32)
            sides = sides.astype(BF16)
            for row in range(MARGIN):
                wide[first + row, :, COLS:] = sides[:, row * COLS : (row + 1) * COLS]
            cells = wide[first : first + MARGIN].reshape(MARGIN * PADDED, 2 * COLS)
            out = jnp.dot(cells, moves[...], preferred_element_type=F32)
            kept[first : first + MARGIN] = out.reshape(MARGIN, PADDED, (KERNEL - 1) * COLS)

    @pl.when(jnp.logical_not(has_above))
    def _():
        for phase in range(2):
            rows_recv[phase, 0] = jnp.zeros((MARGIN, PADDED, COLS), BF16)
            pack_recv[phase, 2] = jnp.zeros((112, COLS), BF16)

    @pl.when(jnp.logical_not(has_below))
    def _():
        for phase in range(2):
            rows_recv[phase, 1] = jnp.zeros((MARGIN, PADDED, COLS), BF16)
            pack_recv[phase, 3] = jnp.zeros((112, COLS), BF16)

    source = iota((2 * COLS, COLS), 0)
    lane = iota((2 * COLS, COLS), 1)
    for column in range(KERNEL):
        if column == MARGIN:
            continue
        wanted = lane + (column - MARGIN)
        beside = (wanted < 0) | (wanted >= COLS)
        wanted = jnp.where(beside, COLS + lax.rem(wanted + COLS, COLS), wanted)
        moves[:, shift_lanes(column)] = (source == wanted).astype(F32).astype(BF16)
    source = iota((COLS, COLS), 0)
    lane = iota((COLS, COLS), 1)
    edge = (lane < MARGIN) | (lane >= COLS - MARGIN)
    for row in range(ROWS):
        hit = edge & (source == lax.rem(lane + 8 * row, COLS))
        turns[:, row * COLS : (row + 1) * COLS] = hit.astype(F32).astype(BF16)

    live = (slot_ref[0] >= 0).astype(F32)
    loads[1].wait()
    loads[0].wait()
    mask = mask_v[...].astype(F32) * live
    flat[...] = (state_v[...].astype(F32) * mask[None]).reshape(CHANNELS * ROWS, COLS)
    for row in range(ROWS):
        ext[MARGIN + row] = flat[pl.ds(row, CHANNELS, stride=ROWS), :]
    pack_up(0, ext)

    met = 2 + (PLACES - 1) + 2 * (CHIPS - 1) + (LINE - 1) * (DEPTH - 1)
    pl.semaphore_wait(barrier, met)

    halo_start_sides(0)
    for copy in loads[2:8]:
        copy.wait()
    vectors = [ref[...].astype(F32).reshape(1, CHANNELS) for ref in (bias_v, gain_v, shift_v, dbias_v, scale_v)]
    lines = [taps_v[...].astype(F32)] + vectors + [jnp.zeros((2, CHANNELS), F32)]
    cols[...] = jnp.concatenate(lines, axis=0).T
    for tap in range(TAPS):
        taps[tap] = jnp.broadcast_to(cols[:, tap : tap + 1], (CHANNELS, COLS))

    halo_start_rest(0, 0)
    loads[8].wait()
    flat[...] = (cot_v[...].astype(F32) * mask[None]).reshape(CHANNELS * ROWS, COLS)
    scale_col = cols[:, SCALE : SCALE + 1]
    for row in range(ROWS):
        masked = flat[pl.ds(row, CHANNELS, stride=ROWS), :]
        mgrad[row] = masked
        gblow[:, row * COLS : (row + 1) * COLS] = (masked * scale_col).astype(BF16)
    for copy in loads[9:]:
        copy.wait()
    bias_line = ubias_v[...].reshape(1, HIDDEN)
    below = jnp.where(iota((PADDED - CHANNELS, HIDDEN), 0) == 0, bias_line.astype(F32), 0.0)
    up_t[...] = jnp.concatenate([upw_v[...], below.astype(BF16)], axis=0)
    up_w[...] = up_t[...].T
    down_t[...] = downw_v[...].T

    fill_inner(ext)
    halo_wait_sides(0)

    move_inner(0)

    @pl.loop(0, BLOCKS, unroll=UNROLL)
    def _(block):
        rows = block_rows(block)
        total = convolve(ext, kept, taps, rows, False, INNER, [None] * ROWS)
        for row in range(ROWS):
            normed[row, rows, :] = total[row]

    halo_wait_rest(0)

    move_outer(0, ext)

    @pl.loop(0, BLOCKS, unroll=UNROLL)
    def _(block):
        rows = block_rows(block)
        total = [normed[row, rows, :] for row in range(ROWS)]
        total = convolve(ext, kept, taps, rows, False, OUTER, total)
        bias = cols[rows, DW_BIAS : DW_BIAS + 1]
        for row in range(ROWS):
            normed[row, rows, :] = (total[row] * live + bias).astype(BF16).astype(F32)

    gain_col = cols[:, GAIN : GAIN + 1]
    shift_col = cols[:, SHIFT : SHIFT + 1]

    @pl.loop(0, ROWS, unroll=ROWS)
    def _(row):
        conv = normed[row]
        offset = conv - jnp.mean(conv, axis=0, keepdims=True)
        rate = lax.rsqrt(jnp.mean(offset * offset, axis=0, keepdims=True) + NORM_EPSILON)
        unit = offset * rate
        spread[row] = rate
        normed[row] = unit
        low = (unit * gain_col + shift_col).astype(BF16)
        tail = (iota((PADDED - CHANNELS, COLS), 0) == 0).astype(F32).astype(BF16)
        nlow[:, lane_slice(row)] = jnp.concatenate([low, tail], axis=0)

    def w_core_copy(part):
        return remote(
            w_send.at[part, 1 - core],
            w_core.at[part],
            core_ssem.at[part],
            core_rsem.at[part],
            g,
            partner,
        )

    def w_line_copy(part, k):
        other = lax.rem((pillar if part == 0 else line) + k, LINE)
        if part == 0:
            gg, tt = lax.rem(other, 2) * LINE + line, (depth * 2 + other // 2) * 2 + core
        else:
            gg, tt = low * LINE + other, t
        return remote(
            w_group.at[part, other],
            w_group_in.at[part, k],
            wgroup_ssem.at[part],
            wgroup_rsem.at[part],
            gg,
            tt,
        )

    def mix(part):
        units = slice(part * CHUNK, (part + 1) * CHUNK)
        pre = jnp.dot(up_w[units, :], nlow[...], preferred_element_type=F32)
        mass = 0.5 * (1.0 + lax.erf(pre * SQRT_HALF))
        density = GAUSS_SCALE * jnp.exp(-0.5 * pre * pre)
        active = (pre * mass).astype(BF16)
        act[units, :] = active
        grad_act = jnp.dot(down_t[units, :], gblow[...], preferred_element_type=F32)
        grad_pre = (grad_act * (mass + pre * density)).astype(BF16)
        gpre[units, :] = grad_pre

    def weight_grads(part):
        units = slice(part * CHUNK, (part + 1) * CHUNK)
        trans = (((1,), (1,)), ((), ()))
        gup[units, :PADDED] = lax.dot_general(
            gpre[units, :], nlow[...], trans, preferred_element_type=F32
        )
        gdown[units, :CHANNELS] = lax.dot_general(
            act[units, :], gblow[...], trans, preferred_element_type=F32
        )
        for tile in range(part * TILES // 2, (part + 1) * TILES // 2):
            for half in range(2):
                begin = tile * SHARE + 16 * half
                for lanes in range(4):
                    source = gup if lanes < 2 else gdown
                    side = (lanes % 2) * COLS
                    piece = source[begin : begin + 16, side : side + COLS]
                    if begin + 16 > HIDDEN:
                        piece = jnp.where(iota((16, COLS), 0) < HIDDEN - begin, piece, 0.0)
                    along, across, spot = half * 2 + lanes // 2, lanes % 2, tile // 2
                    if part == 0:
                        first, second = spot % 2 * 2 + across, along * 4 + spot // 2
                    else:
                        first, second = along, across * 8 + spot - 8
                    w_send[part, tile % 2, first, second] = piece.astype(BF16)
        w_core_copy(part).start()

    def weight_share(part):
        finished(w_core_copy(part))

        @pl.loop(0, LINE)
        def _(piece):
            total = w_send[part, core, piece].astype(F32) + w_core[part, piece].astype(F32)
            w_group[part, piece] = total.astype(BF16)

        for k in range(1, LINE):
            w_line_copy(part, k).start()

    mix(0)

    weight_grads(0)

    mix(1)

    weight_share(0)

    branch[...] = jnp.dot(downw_v[...], act[...], preferred_element_type=F32)
    gnorm[...] = jnp.dot(up_t[...], gpre[...], preferred_element_type=F32)[:CHANNELS]

    sums[...] = jnp.zeros_like(sums)
    down_bias = cols[:, DOWN_BIAS : DOWN_BIAS + 1]

    @pl.loop(0, ROWS, unroll=4)
    def _(row):
        grad = gnorm[:, lane_slice(row)]
        unit = normed[row]
        masked = mgrad[row]
        sums[1] += grad * unit
        sums[2] += grad
        sums[3] += masked * scale_col
        sums[4] += masked * (branch[:, lane_slice(row)] + down_bias)
        scaled = grad * gain_col
        first = jnp.mean(scaled, axis=0, keepdims=True)
        second = jnp.mean(scaled * unit, axis=0, keepdims=True)
        low = (spread[row] * (scaled - first - unit * second)).astype(BF16).astype(F32)
        exg[MARGIN + row] = low
        sums[0] += low

    pack_up(1, exg)
    halo_start_sides(1)

    weight_grads(1)
    halo_start_rest(1, 0)

    def tap_block(block):
        rows = block_rows(block)
        lane = iota((8, COLS), 1)
        own = [exg[MARGIN + row, rows, :] for row in range(ROWS)]
        out = jnp.zeros((8, COLS), F32)
        for column in range(KERNEL):
            moved = [moved_row(ext, kept, row, rows, column) for row in range(TALL)]
            for tap_row in range(KERNEL):
                total = own[0] * moved[tap_row]
                for row in range(1, ROWS):
                    total = total + own[row] * moved[row + tap_row]
                spot = lane == tap_row * KERNEL + column
                out = jnp.where(spot, jnp.sum(total, axis=1, keepdims=True), out)
        for vector in range(5):
            total = jnp.sum(sums[vector, rows, :], axis=1, keepdims=True)
            out = jnp.where(lane == TAPS + vector, total, out)
        small_wide[rows, :] = out * live

    pl.loop(0, BLOCKS, unroll=UNROLL)(tap_block)

    second = pltpu.roll(small_wide[FOLD:], 64, 1)
    whole = jnp.concatenate(
        [
            small_wide[: CHANNELS - FOLD] + second,
            small_wide[CHANNELS - FOLD : FOLD],
            jnp.zeros((128 - FOLD, COLS), F32),
        ],
        axis=0,
    )
    small[...] = whole.reshape(PLACES, 8, COLS)

    def s_copy(k):
        gg, tt, other = other_place(k)
        return remote(small.at[other], small_in.at[k], small_ssem, small_rsem, gg, tt)

    for k in range(1, PLACES):
        s_copy(k).start()

    weight_share(1)

    fill_inner(exg)
    halo_wait_sides(1)

    move_inner(1)

    def finish_inner(block):
        rows = block_rows(block)
        total = convolve(exg, kept, taps, rows, True, INNER, [None] * ROWS)
        for row in range(ROWS):
            gstate[row, rows, :] = total[row]

    def finish_outer(block):
        rows = block_rows(block)
        total = [gstate[row, rows, :] for row in range(ROWS)]
        total = convolve(exg, kept, taps, rows, True, OUTER, total)
        for row in range(ROWS):
            cell = mask[row : row + 1]
            spots = pl.ds(block * 64 + row, 8, stride=ROWS)
            flat[spots, :] = cell * (mgrad[row, rows, :] + total[row])

    near = line * 4 + lax.rem(depth, 4)
    far = low * 8 + lax.rem(chip, 8)

    def w_tile_copy(part, k):
        if part == 0:
            other = lax.rem(near + k, 16)
            gg, tt = low * LINE + other // 4, (lax.rem(other, 4) * 2 + high) * 2 + core
        else:
            other = lax.rem(far + k, 16)
            gg, tt = other // 8 * LINE + line, (8 + lax.rem(other, 8)) * 2 + core
        return remote(
            w_tile.at[part, other],
            w_tile_in.at[sheet if part == 0 else plane],
            wtile_ssem,
            wtile_rsem,
            gg,
            tt,
        )

    def w_piece_sums(part):
        total = w_group[part, pillar if part == 0 else line].astype(F32)
        all_finished(w_group_in.at[part], LINE - 1, wgroup_ssem.at[part], wgroup_rsem.at[part])
        for k in range(1, LINE):
            total = total + w_group_in[part, k].astype(F32)
        w_tile[part] = total.astype(BF16)

        @pl.when(upper != part)
        def _():
            w_tile_copy(part, 0).start()

        for k in range(1, 16):
            w_tile_copy(part, k).start()

    pl.loop(0, 15, unroll=UNROLL)(finish_inner)

    w_piece_sums(0)

    total = small[place]
    all_finished(small_in, PLACES - 1, small_ssem, small_rsem)
    for k in range(1, PLACES):
        total = total + small_in[k]
    s_tile[...] = total

    def s_tile_copy(k):
        other = lax.rem(chip + k, CHIPS)
        return remote(
            s_tile, s_tile_in.at[chip], stile_ssem, stile_rsem, g, other * 2 + core
        )

    for k in range(1, CHIPS):
        s_tile_copy(k).start()

    pl.loop(15, BLOCKS, unroll=UNROLL)(finish_inner)

    w_piece_sums(1)

    halo_wait_rest(1)

    move_outer(1, exg)

    pl.loop(0, BLOCKS, unroll=UNROLL)(finish_outer)

    state_v[...] = flat[...].reshape(CHANNELS, ROWS, COLS).astype(BF16)
    store = pltpu.make_async_copy(state_v, gs_ref, store_sem)
    store.start()

    w_tile_in[upper * plane + (1 - upper) * sheet] = w_tile[upper, upper * far + (1 - upper) * near]
    all_finished(w_tile_in, PLANE - 1, wtile_ssem, wtile_rsem)
    total = w_tile_in[0].astype(F32)
    for other in range(1, PLANE):
        total = total + w_tile_in[other].astype(F32)
    piece = line * 2 + low
    w_final[piece] = total

    def w_final_copy(k):
        other = lax.rem(g + k, GROUPS)
        return remote(
            w_final.at[piece], w_final.at[piece], wfinal_ssem, wfinal_rsem, other, t
        )

    for k in range(1, GROUPS):
        w_final_copy(k).start()

    s_tile_in[chip] = s_tile[...]
    all_finished(s_tile_in, CHIPS - 1, stile_ssem, stile_rsem)
    total = s_tile_in[0]
    for other in range(1, CHIPS):
        total = total + s_tile_in[other]
    s_final[place] = total

    def s_final_copy(k):
        gg, tt, _ = other_place(k)
        return remote(
            s_final.at[place], s_final.at[place], sfinal_ssem, sfinal_rsem, gg, tt
        )

    for k in range(1, PLACES):
        s_final_copy(k).start()

    all_finished(w_final, GROUPS - 1, wfinal_ssem, wfinal_rsem)
    all_finished(s_final, PLACES - 1, sfinal_ssem, sfinal_rsem)
    factor = 1.0 / math.sqrt(CELLS * GROUPS * TILES)
    tail_ref[0] = w_final[...].reshape(128, COLS) * factor
    tail_ref[1] = s_final[...].reshape(128, COLS) * factor
    store.wait()


def scratch():
    dma = pltpu.SemaphoreType.DMA
    tile = (CHANNELS, ROWS, COLS)
    rows = (ROWS, CHANNELS, COLS)
    tall = (TALL, CHANNELS, COLS)
    pieces = (LINE, 16, 16, COLS)
    return [
        pltpu.VMEM((ROWS, COLS), jnp.int32),
        pltpu.VMEM(tile, BF16),
        pltpu.VMEM(tile, BF16),
        pltpu.VMEM((TAPS, CHANNELS), BF16),
        pltpu.VMEM((CHANNELS, HIDDEN), BF16),
        pltpu.VMEM((CHANNELS, HIDDEN), BF16),
        pltpu.VMEM((CHANNELS,), BF16),
        pltpu.VMEM((CHANNELS,), BF16),
        pltpu.VMEM((CHANNELS,), BF16),
        pltpu.VMEM((CHANNELS,), BF16),
        pltpu.VMEM((CHANNELS,), BF16),
        pltpu.VMEM((HIDDEN,), BF16),
        pltpu.VMEM((CHANNELS, 56), F32),
        pltpu.VMEM((2 * COLS, (KERNEL - 1) * COLS), BF16),
        pltpu.VMEM((COLS, ROWS * COLS), BF16),
        pltpu.VMEM((CHANNELS * ROWS, COLS), F32),
        pltpu.VMEM(tall, F32),
        pltpu.VMEM(tall, F32),
        pltpu.VMEM((TALL, PADDED, 2 * COLS), BF16),
        pltpu.VMEM((TAPS, CHANNELS, COLS), F32),
        pltpu.VMEM((TALL, PADDED, (KERNEL - 1) * COLS), F32),
        pltpu.VMEM(rows, F32),
        pltpu.VMEM((ROWS, 1, COLS), F32),
        pltpu.VMEM(rows, F32),
        pltpu.VMEM((PADDED, CELLS), BF16),
        pltpu.VMEM((CHANNELS, CELLS), BF16),
        pltpu.VMEM((HIDDEN, CELLS), BF16),
        pltpu.VMEM((HIDDEN, CELLS), BF16),
        pltpu.VMEM((CHANNELS, CELLS), F32),
        pltpu.VMEM((CHANNELS, CELLS), F32),
        pltpu.VMEM((PADDED, HIDDEN), BF16),
        pltpu.VMEM((HIDDEN, PADDED), BF16),
        pltpu.VMEM((HIDDEN, CHANNELS), BF16),
        pltpu.VMEM((HIDDEN + 8, 256), F32),
        pltpu.VMEM((HIDDEN + 8, 256), F32),
        pltpu.VMEM((5, CHANNELS, COLS), F32),
        pltpu.VMEM((CHANNELS, COLS), F32),
        pltpu.VMEM(rows, F32),
        pltpu.VMEM((2, 2, MARGIN, PADDED, COLS), BF16),
        pltpu.VMEM((2, 2, MARGIN, PADDED, COLS), BF16),
        pltpu.VMEM((2, 2, 112, COLS), BF16),
        pltpu.VMEM((2, 4, 112, COLS), BF16),
        pltpu.VMEM((2, 2) + pieces, BF16),
        pltpu.VMEM((2,) + pieces, BF16),
        pltpu.VMEM((2,) + pieces, BF16),
        pltpu.VMEM((2,) + pieces, BF16),
        pltpu.VMEM((2, 16, 16, COLS), BF16),
        pltpu.VMEM((PLANE, 16, COLS), BF16),
        pltpu.VMEM((GROUPS, 16, COLS), F32),
        pltpu.VMEM((PLACES, 8, COLS), F32),
        pltpu.VMEM((PLACES, 8, COLS), F32),
        pltpu.VMEM((8, COLS), F32),
        pltpu.VMEM((CHIPS, 8, COLS), F32),
        pltpu.VMEM((PLACES, 8, COLS), F32),
        dma((12,)),
        dma(()),
        dma((2, 6)),
        dma((2, 6)),
        dma((2,)),
        dma((2,)),
        dma((2,)),
        dma((2,)),
        dma(()),
        dma(()),
        dma(()),
        dma(()),
        dma(()),
        dma(()),
        dma(()),
        dma(()),
        dma(()),
        dma(()),
    ]


def place_results(rows_ref, tail_ref, gs_ref, up_ref, ubias_ref, down_ref, taps_ref, vec_ref, sem):
    copy = pltpu.make_async_copy(rows_ref, gs_ref, sem)
    copy.start()
    for half, size in ((0, 16), (1, SHARE - 16)):
        for part in range(4):
            piece = tail_ref[0, (half * 4 + part) * 16 : (half * 4 + part) * 16 + size, :]
            target = up_ref if part < 2 else down_ref
            begin = (part % 2) * COLS
            width = min(COLS, CHANNELS - begin)
            target[half * 16 : half * 16 + size, begin : begin + width] = piece[:, :width]
    edge = jnp.concatenate([tail_ref[0, 16:32, :], tail_ref[0, 80:96, :]], axis=0)
    line = edge.T[CHANNELS - COLS : CHANNELS - COLS + 1, :SHARE]
    ubias_ref[...] = line.reshape(SHARE)
    turned = tail_ref[1].T
    low, high = turned[:64, :FOLD], turned[64:, : CHANNELS - FOLD]
    every = jnp.concatenate([low, high], axis=1)
    taps_ref[...] = every[:TAPS]
    vec_ref[...] = every[TAPS : TAPS + 5]
    copy.wait()


def local(
    state_in,
    cotangent,
    ocean_mask,
    slot_column,
    dw_taps,
    dw_bias,
    norm_gain,
    norm_bias,
    up_weight,
    up_bias,
    down_weight,
    down_bias,
    layer_scale,
):
    vmem = pl.BlockSpec(memory_space=pltpu.VMEM)
    anywhere = pl.BlockSpec(memory_space=pl.ANY)
    grad_rows, tail = pl.pallas_call(
        kernel,
        out_shape=(
            jax.ShapeDtypeStruct((CHANNELS, ROWS, COLS), BF16),
            jax.ShapeDtypeStruct((2, 128, COLS), F32),
        ),
        in_specs=[pl.BlockSpec(memory_space=pltpu.SMEM)] + [anywhere] * 12,
        out_specs=(anywhere, vmem),
        scratch_shapes=scratch(),
        compiler_params=pltpu.CompilerParams(
            collective_id=0, has_side_effects=True, vmem_limit_bytes=VMEM_BYTES
        ),
    )(
        slot_column,
        ocean_mask[0],
        state_in[0],
        cotangent[0],
        dw_taps.T,
        up_weight.T,
        down_weight,
        dw_bias,
        norm_gain,
        norm_bias,
        down_bias,
        layer_scale,
        up_bias,
    )
    grad_state, grad_up, grad_up_bias, grad_down, grad_taps, grad_vectors = pl.pallas_call(
        place_results,
        out_shape=(
            jax.ShapeDtypeStruct((CHANNELS, ROWS, COLS), BF16),
            jax.ShapeDtypeStruct((SHARE, CHANNELS), F32),
            jax.ShapeDtypeStruct((SHARE,), F32),
            jax.ShapeDtypeStruct((SHARE, CHANNELS), F32),
            jax.ShapeDtypeStruct((TAPS, CHANNELS), F32),
            jax.ShapeDtypeStruct((5, CHANNELS), F32),
        ),
        in_specs=[vmem, vmem],
        out_specs=(anywhere,) + (vmem,) * 5,
        scratch_shapes=[pltpu.SemaphoreType.DMA(())],
    )(grad_rows, tail)
    return grad_state[None], grad_up, grad_up_bias, grad_down.T, grad_taps.T, grad_vectors


def solution(mesh):
    slots = P(("group", "tile"), None, None, None)
    in_specs = (slots, slots, P(("group", "tile"), None, None), P(("group", "tile"))) + (P(),) * 9
    out_specs = (slots, P("tile", None), P("tile"), P(None, "tile"), P(), P())
    return jax.shard_map(local, mesh=mesh, in_specs=in_specs, out_specs=out_specs, check_vma=False)
```
